1024 devices in a mesh: dp: 32 (over y, x), expert: 32 (over z, core).
Axes of the slice: x: 4, y: 8, z: 16, core: 2. Of those that a mesh axis runs over, the one named last changes fastest.
Arguments:
- latent: bfloat16 [131072, 512], P(('dp', 'expert')), may hold values from -6 to 6
- up_proj: bfloat16 [512, 4096], P(None, 'expert'), may hold values from -0.25 to 0.25
- expert_in: bfloat16 [32, 512, 4096], P('expert'), may hold values from -0.25 to 0.25
- expert_out: bfloat16 [32, 2048, 512], P('expert'), may hold values from -0.125 to 0.125
- routes: int32 [131072, 8], P(('dp', 'expert')), may hold values from 0 to 127, all different within a row; in each aligned block of 128 rows (0 to 127, 128 to 255, ...) at most 13 rows name the same one
- gates: bfloat16 [131072, 8], P(('dp', 'expert')), may hold values from 0.099609375 to 1
- cotangent: bfloat16 [131072, 4096], P('dp', 'expert'), may hold values from -6 to 6
Outputs:
- mixed: bfloat16 [131072, 4096], P('dp', 'expert')
- grad_up: float32 [512, 4096], P(None, 'expert')
The draws below stay inside these ranges and needn't reach their ends.
Inputs may be any that keep to these rules, and one draw needn't show every extreme that they name: `routes`: in each aligned block of 128 rows (the tokens of one device) no expert is named more than 13 times.
All inputs are finite; a program needn't handle non-finite values.
Results may differ from the reference program's by a relative error of at most 0.0064.
Values may be sent and summed in bfloat16 or wider, within the bound.
No kernel may reach another device: no remote copies, remote signals or barrier semaphores. Data moves between devices by JAX's collectives and lax.ppermute only.
A program may use at most 32 MiB of HBM per device.

```python
import math
import jax
import jax.numpy as jnp
import numpy as np
from jax import lax

D = 4096
L = 512
H = 2048
EXPERTS = 128
TOP = 8
TOK_DEV = 128
CAP = 13
FLY = 32
TOKENS = 131072


def levels(own_key, extent, shards, smallest, largest):
    def one(position, shards_of):
        heights = jax.random.uniform(jax.random.fold_in(jax.random.fold_in(own_key, 6), position), (shards_of,), jnp.float32, smallest / len(shards), largest / len(shards))
        return jnp.repeat(jnp.exp(heights), extent[position] // shards_of).reshape((-1,) + (1,) * (len(extent) - position - 1))

    gain = one(*shards[0])
    for cut in shards[1:]:
        gain = gain * one(*cut)
    return gain


def routed_block(rng, own, number, rows, count, top, most, slope):
    sequence = jax.random.permutation(rng, count)
    heavy_load, usual = load_shares(count, rows * top, most, slope, True), load_shares(count, rows * top, most, slope, False)
    places = jnp.arange(count)

    def named(tallies, rotation):
        used = int((tallies > 0).sum())
        fixed = max(1, used // 4)
        shifted = fixed + (places - fixed + rotation * (used - fixed)) % max(1, count - fixed)
        return jnp.zeros((count,), jnp.int32).at[sequence[jnp.where(places < fixed, places, shifted)]].set(jnp.asarray(tallies, jnp.int32))

    tallies = jnp.where(number % 4 == 0, named(heavy_load, number // 4), named(usual, number - number // 4 - 1))
    mixed = jax.random.permutation(jax.random.fold_in(own, 3), count)
    giver, sink = mixed[0:count // 2 * 2:2], mixed[1:count // 2 * 2:2]
    room = jnp.minimum(tallies[giver] - 1, most - tallies[sink]) // 2
    room = jnp.where((giver == sequence[0]) | (sink == sequence[0]) | (tallies[sink] == 0), 0, jnp.maximum(room, 0))
    shifted = jax.random.randint(jax.random.fold_in(own, 4), (count // 2,), 0, 1 << 20) % (room + 1)
    tallies = tallies.at[giver].add(-shifted).at[sink].add(shifted)
    members = jnp.searchsorted(jnp.cumsum(tallies), jnp.arange(rows * top), side="right").astype(jnp.int32)
    listing = members.reshape(top, rows).T
    listing = listing[jax.random.permutation(jax.random.fold_in(own, 1), rows)]
    rotation = jax.random.randint(jax.random.fold_in(own, 2), (rows, 1), 0, top)
    return jnp.take_along_axis(listing, (jnp.arange(top)[None, :] + rotation) % top, axis=1)


def load_shares(number_of, total, bound, slope, full):
    portions = [(1 << 20) // math.isqrt(standing ** slope) + 1 for standing in range(1, number_of + 1)]
    largest = bound if full else min(bound, max(-(-total // number_of), total * portions[0] // sum(portions)))
    least = 1 if total - largest >= number_of - 1 else 0
    holding, surplus = [largest] + [least] * (number_of - 1), total - largest - least * (number_of - 1)
    while surplus > 0:
        movable = [i for i in range(1, number_of) if holding[i] < largest] or [i for i in range(1, number_of) if holding[i] < bound]
        pool, budget = sum([portions[i] for i in movable]), surplus
        for i in movable:
            extra = min(bound - holding[i], max(1, budget * portions[i] // pool), surplus)
            holding[i] = holding[i] + extra
            surplus = surplus - extra
    return np.array(holding)


def normal_values(own_key, shape, width, limit, pieces=(), kind=jnp.bfloat16):
    result = width * jax.random.normal(own_key, shape, jnp.float32)
    if pieces:
        result = result * levels(own_key, shape, pieces, -0.22, 0.18)
    return jnp.clip(result, -limit, limit).astype(kind)


def setup_inputs(seed: int = 0) -> dict:
    key_list = jax.random.split(jax.random.key(seed), 8)
    latent = normal_values(key_list[0], (TOKENS, L), 1.0, 6.0, ((0, 1024),))
    up_proj = normal_values(key_list[1], (L, D), L ** -0.5, 0.25, ((1, 32),))
    expert_in = normal_values(key_list[2], (FLY, L, 2 * H), L ** -0.5, 0.25, ((0, 32),))
    expert_out = normal_values(key_list[3], (FLY, H, L), H ** -0.5, 0.125, ((0, 32),))
    routes_keys = jax.random.split(jax.random.fold_in(key_list[4], 1), TOKENS // TOK_DEV)
    routes_turns = jax.random.permutation(jax.random.fold_in(key_list[4], 3), TOKENS // TOK_DEV)
    routes = jax.vmap(lambda own, number: routed_block(jax.random.fold_in(key_list[4], 2), own, number, TOK_DEV, EXPERTS, TOP, CAP, 2))(routes_keys, routes_turns).reshape((TOKENS, TOP))
    gates = jnp.clip(jnp.exp(math.log(1.0) - 2.306499 * jax.random.uniform(key_list[5], (TOKENS, TOP), jnp.float32) ** levels(key_list[5], (TOKENS, TOP), ((0, 1024),), -0.2, 0.2)), 0.099609375, 1.0).astype(jnp.bfloat16)
    cotangent = normal_values(key_list[6], (TOKENS, D), 1.0, 6.0, ((0, 32), (1, 32)))
    return dict(latent=latent, up_proj=up_proj, expert_in=expert_in, expert_out=expert_out, routes=routes, gates=gates, cotangent=cotangent)


def run_expert(item):
    arrived, weight_in, weight_out = item
    hidden = weight_out.shape[0]
    gated = jnp.dot(arrived, weight_in, preferred_element_type=jnp.float32)
    act = (jax.nn.silu(gated[:, :hidden]) * gated[:, hidden:]).astype(jnp.bfloat16)
    return jnp.dot(act, weight_out, preferred_element_type=jnp.float32).astype(jnp.bfloat16)


def reference(latent, up_proj, expert_in, expert_out, routes, gates, cotangent):
    blocks = TOKENS // TOK_DEV
    flat = routes.reshape(blocks, TOK_DEV * TOP).astype(jnp.int32)
    onehot = (flat[:, :, None] == jnp.arange(FLY, dtype=jnp.int32)[None, None, :]).astype(jnp.int32)
    before = jnp.cumsum(onehot, axis=1).astype(jnp.int32) - onehot
    slot = jnp.sum(before * onehot, axis=2).astype(jnp.int32)
    inside = (flat < FLY).reshape(-1)
    row = (jnp.arange(blocks, dtype=jnp.int32)[:, None] * CAP + slot).reshape(-1).astype(jnp.int32)
    which = jnp.where(inside, flat.reshape(-1), FLY).astype(jnp.int32)
    source = jnp.repeat(latent, TOP, axis=0)
    buffers = jnp.zeros((FLY, blocks * CAP, L), jnp.bfloat16).at[which, row].set(source, mode="drop")
    outputs = lax.map(run_expert, (buffers, expert_in, expert_out))
    picked = outputs[jnp.minimum(which, FLY - 1), row].astype(jnp.float32)
    weight = jnp.where(inside, gates.reshape(-1).astype(jnp.float32), jnp.float32(0.0))
    combined = jnp.sum((picked * weight[:, None]).reshape(TOKENS, TOP, L), axis=1).astype(jnp.bfloat16)
    mixed = jnp.dot(combined, up_proj, preferred_element_type=jnp.float32).astype(jnp.bfloat16)
    grad_up = jnp.dot(combined.T, cotangent, preferred_element_type=jnp.float32)
    return mixed, grad_up
```

```python
import jax
import jax.numpy as jnp
from jax import lax
from jax.experimental import pallas as pl
from jax.experimental.pallas import tpu as pltpu
from jax.sharding import PartitionSpec as P

SLOTS = 16
BF16, F32 = jnp.bfloat16, jnp.float32
VMEM = pl.BlockSpec(memory_space=pltpu.VMEM)
LIMIT = pltpu.CompilerParams(vmem_limit_bytes=48 << 20)


def iota(shape, dim):
    return lax.broadcasted_iota(jnp.int32, shape, dim)


def slots_by_row(routes_t, n_expert):
    top, tok = routes_t.shape
    expert = iota((n_expert, tok), 0)
    member = jnp.zeros((n_expert, tok), F32)
    for k in range(top):
        member += jnp.where(routes_t[k : k + 1, :] == expert, 1.0, 0.0)
    earlier = jnp.where(iota((tok, tok), 0) < iota((tok, tok), 1), 1.0, 0.0).astype(BF16)
    slot = jnp.dot(member.astype(BF16), earlier, preferred_element_type=F32)
    slot = jnp.where(member > 0, slot, -1.0).astype(BF16)
    rows = n_expert * SLOTS
    spread = jnp.where(iota((rows, n_expert), 0) // SLOTS == iota((rows, n_expert), 1), 1.0, 0.0).astype(BF16)
    by_row = jnp.dot(spread, slot, preferred_element_type=F32)
    return by_row == (iota((rows, tok), 0) % SLOTS).astype(F32), spread


def dispatch_kernel(routes_ref, latent_ref, out_ref):
    n_expert = out_ref.shape[0] // SLOTS
    takes, _ = slots_by_row(routes_ref[...], n_expert)
    out_ref[...] = jnp.dot(
        jnp.where(takes, 1.0, 0.0).astype(BF16), latent_ref[...], preferred_element_type=F32
    ).astype(BF16)


def weight_kernel(routes_ref, gates_ref, out_ref):
    n_expert = out_ref.shape[1] // SLOTS
    routes_t, gates_t = routes_ref[...], gates_ref[...].astype(F32)
    takes, spread = slots_by_row(routes_t, n_expert)
    top, tok = routes_t.shape
    expert = iota((n_expert, tok), 0)
    gate = jnp.zeros((n_expert, tok), F32)
    for k in range(top):
        gate += jnp.where(routes_t[k : k + 1, :] == expert, gates_t[k : k + 1, :], 0.0)
    by_row = jnp.dot(spread, gate.astype(BF16), preferred_element_type=F32)
    out_ref[...] = jnp.where(takes, by_row, 0.0).T.astype(BF16)


def expert_kernel(x_ref, in_ref, out_w_ref, out_ref):
    hidden = out_w_ref.shape[0]
    step = 512
    x = x_ref[...]
    total = jnp.zeros(out_ref.shape, F32)
    for h in range(0, hidden, step):
        g = jnp.dot(x, in_ref[:, h : h + step], preferred_element_type=F32)
        u = jnp.dot(x, in_ref[:, hidden + h : hidden + h + step], preferred_element_type=F32)
        act = (g / (1.0 + jnp.exp(-g)) * u).astype(BF16)
        total += jnp.dot(act, out_w_ref[h : h + step, :], preferred_element_type=F32)
    out_ref[...] = total.astype(BF16)


def combine_kernel(w_ref, back_ref, out_ref):
    out_ref[...] = jnp.dot(w_ref[...], back_ref[...], preferred_element_type=F32).astype(BF16)


def project_kernel(core_ref, rows_ref, up_ref, cot_ref, *rest):
    before_ref = rest[0] if len(rest) == 5 else None
    mixed_ref, grad_ref, total = rest[-3:]
    i = pl.program_id(0)
    many, tok, width = rows_ref.shape
    rows = rows_ref[...].reshape(many * tok, width)
    cot = cot_ref[...].reshape(many * tok, -1)
    mixed = jnp.dot(rows, up_ref[...], preferred_element_type=F32).astype(BF16)
    mixed_ref[...] = mixed.reshape(mixed_ref.shape)
    part = lax.dot_general(rows, cot, (((0,), (0,)), ((), ())), preferred_element_type=F32)

    @pl.when(i == 0)
    def _():
        total[...] = part if before_ref is None else part + before_ref[...]

    @pl.when(i > 0)
    def _():
        total[...] += part

    @pl.when(i == pl.num_programs(0) - 1)
    def _():
        grad_ref[...] = total[...].astype(grad_ref.dtype)


def project(core, rows, up_proj, cot4, grad=None, mixed=None):
    z, tok, width = rows.shape
    cols = up_proj.shape[1]
    many = z // 4
    first = grad is None
    whole = pl.BlockSpec((width, cols), lambda i, c: (0, 0))
    mine = pl.BlockSpec((many, 1, tok, cols), lambda i, c: (i, c[0], 0, 0))
    in_specs = [pl.BlockSpec((many, tok, width), lambda i, c: (i, 0, 0)), whole, mine]
    args = [core, rows, up_proj, cot4]
    if not first:
        in_specs += [whole, pl.BlockSpec(memory_space=pl.ANY)]
        args += [grad, mixed]
    return pl.pallas_call(
        project_kernel,
        grid_spec=pltpu.PrefetchScalarGridSpec(
            num_scalar_prefetch=1,
            grid=(z // many,),
            in_specs=in_specs,
            out_specs=[mine, whole],
            scratch_shapes=[pltpu.VMEM((width, cols), F32)],
        ),
        out_shape=[
            jax.ShapeDtypeStruct(cot4.shape, BF16),
            jax.ShapeDtypeStruct((width, cols), F32 if first else BF16),
        ],
        input_output_aliases={} if first else {5: 0},
        compiler_params=LIMIT,
        cost_estimate=pl.CostEstimate(flops=4 * z * tok * width * cols, bytes_accessed=4 << 20, transcendentals=0),
        name="project_own" if first else "project_other",
    )(*args)


def body(latent, up_proj, expert_in, expert_out, routes, gates, cotangent):
    n_expert = lax.axis_size("expert")
    n_dp = lax.axis_size("dp")
    tok, width = latent.shape
    cols = up_proj.shape[1]
    nz = n_expert // 2
    slots = n_expert * SLOTS
    same_core = [[z * 2 + c for z in range(nz)] for c in range(2)]
    sds = jax.ShapeDtypeStruct

    routes_t, gates_t = routes.T, gates.T
    outgoing = pl.pallas_call(
        dispatch_kernel, out_shape=sds((slots, width), BF16), in_specs=[VMEM] * 2, out_specs=VMEM, name="dispatch"
    )(routes_t, latent)
    weight = pl.pallas_call(
        weight_kernel, out_shape=sds((tok, slots), BF16), in_specs=[VMEM] * 2, out_specs=VMEM, name="weight"
    )(routes_t, gates_t)
    arrived = lax.all_to_all(
        outgoing.reshape(n_expert, SLOTS, width), "expert", split_axis=0, concat_axis=0, tiled=True
    ).reshape(slots, width)
    produced = pl.pallas_call(
        expert_kernel, out_shape=sds((slots, width), BF16), in_specs=[VMEM] * 3, out_specs=VMEM,
        compiler_params=LIMIT, name="expert",
    )(arrived, expert_in[0], expert_out[0])
    back = lax.all_to_all(
        produced.reshape(n_expert, SLOTS, width), "expert", split_axis=0, concat_axis=0, tiled=True
    ).reshape(slots, width)
    combined = pl.pallas_call(
        combine_kernel, out_shape=sds((tok, width), BF16), in_specs=[VMEM] * 2, out_specs=VMEM, name="combine"
    )(weight, back)

    own = lax.all_gather(combined, "expert", axis=0, tiled=True, axis_index_groups=same_core)
    other = lax.ppermute(own, "expert", [(d, d ^ 1) for d in range(n_expert)])
    core = lax.rem(lax.axis_index("expert"), 2).astype(jnp.int32).reshape(1)
    cot4 = cotangent.reshape(nz, 2, tok, cols)
    mixed, grad = project(core, own.reshape(nz, tok, width), up_proj, cot4)
    mixed, grad = project(1 - core, other.reshape(nz, tok, width), up_proj, cot4, grad, mixed)

    parts = lax.all_to_all(grad.reshape(n_dp, width // n_dp, cols), "dp", split_axis=0, concat_axis=0, tiled=True)
    mine = jnp.sum(parts.astype(F32), axis=0)
    spread = jnp.broadcast_to(mine[None], (n_dp,) + mine.shape)
    grad_up = lax.all_to_all(spread, "dp", split_axis=0, concat_axis=0, tiled=True)
    return mixed.reshape(cotangent.shape), grad_up.reshape(width, cols)


def solution(mesh):
    in_specs = (
        P(("dp", "expert"), None),
        P(None, "expert"),
        P("expert", None, None),
        P("expert", None, None),
        P(("dp", "expert"), None),
        P(("dp", "expert"), None),
        P("dp", "expert"),
    )
    out_specs = (P("dp", "expert"), P(None, "expert"))
    return jax.shard_map(body, mesh=mesh, in_specs=in_specs, out_specs=out_specs, check_vma=False)
```

```python
import jax
import jax.numpy as jnp
from jax import lax
from jax.experimental import pallas as pl
from jax.experimental.pallas import tpu as pltpu
from jax.sharding import PartitionSpec as P

SLOTS = 16
EXTRA = 8
BF16, F32 = jnp.bfloat16, jnp.float32
VMEM = pl.BlockSpec(memory_space=pltpu.VMEM)
LIMIT = pltpu.CompilerParams(vmem_limit_bytes=48 << 20)


def iota(shape, dim):
    return lax.broadcasted_iota(jnp.int32, shape, dim)


def slots_by_row(routes_t, n_expert):
    top, tok = routes_t.shape
    expert = iota((n_expert, tok), 0)
    member = jnp.zeros((n_expert, tok), F32)
    for k in range(top):
        member += jnp.where(routes_t[k : k + 1, :] == expert, 1.0, 0.0)
    earlier = jnp.where(iota((tok, tok), 0) < iota((tok, tok), 1), 1.0, 0.0).astype(BF16)
    slot = jnp.dot(member.astype(BF16), earlier, preferred_element_type=F32)
    slot = jnp.where(member > 0, slot, -1.0).astype(BF16)
    rows = n_expert * SLOTS
    spread = jnp.where(iota((rows, n_expert), 0) // SLOTS == iota((rows, n_expert), 1), 1.0, 0.0).astype(BF16)
    by_row = jnp.dot(spread, slot, preferred_element_type=F32)
    return by_row == (iota((rows, tok), 0) % SLOTS).astype(F32), spread


def dispatch_kernel(routes_ref, latent_ref, out_ref):
    n_expert = out_ref.shape[0] // SLOTS
    takes, _ = slots_by_row(routes_ref[...], n_expert)
    out_ref[...] = jnp.dot(
        jnp.where(takes, 1.0, 0.0).astype(BF16), latent_ref[...], preferred_element_type=F32
    ).astype(BF16)


def weight_kernel(routes_ref, gates_ref, out_ref):
    n_expert = out_ref.shape[1] // SLOTS
    routes_t, gates_t = routes_ref[...], gates_ref[...].astype(F32)
    takes, spread = slots_by_row(routes_t, n_expert)
    top, tok = routes_t.shape
    expert = iota((n_expert, tok), 0)
    gate = jnp.zeros((n_expert, tok), F32)
    for k in range(top):
        gate += jnp.where(routes_t[k : k + 1, :] == expert, gates_t[k : k + 1, :], 0.0)
    by_row = jnp.dot(spread, gate.astype(BF16), preferred_element_type=F32)
    out_ref[...] = jnp.where(takes, by_row, 0.0).T.astype(BF16)


def expert_kernel(x_ref, in_hbm, out_hbm, out_ref, in_ref, out_w_ref, sems):
    hidden = out_w_ref.shape[0]
    step = hidden // sems.shape[0]
    copies = []
    for n in range(sems.shape[0]):
        gate, up = pl.ds(n * step, step), pl.ds(hidden + n * step, step)
        group = [
            pltpu.make_async_copy(in_hbm.at[:, gate], in_ref.at[:, gate], sems.at[n, 0]),
            pltpu.make_async_copy(in_hbm.at[:, up], in_ref.at[:, up], sems.at[n, 1]),
            pltpu.make_async_copy(out_hbm.at[gate, :], out_w_ref.at[gate, :], sems.at[n, 2]),
        ]
        for copy in group:
            copy.start()
        copies.append(group)
    x = x_ref[...]
    total = jnp.zeros(out_ref.shape, F32)
    for n, group in enumerate(copies):
        h = n * step
        group[0].wait()
        g = jnp.dot(x, in_ref[:, h : h + step], preferred_element_type=F32)
        group[1].wait()
        u = jnp.dot(x, in_ref[:, hidden + h : hidden + h + step], preferred_element_type=F32)
        act = (g / (1.0 + jnp.exp(-g)) * u).astype(BF16)
        group[2].wait()
        total += jnp.dot(act, out_w_ref[h : h + step, :], preferred_element_type=F32)
    out_ref[...] = total.astype(BF16)


def power(e):
    return jnp.exp2(e).astype(BF16)


def combine_kernel(w_ref, back_ref, out_ref):
    tok = w_ref.shape[0]
    combined = jnp.dot(w_ref[...], back_ref[...], preferred_element_type=F32).astype(BF16).astype(F32)
    largest = jnp.maximum(jnp.max(jnp.abs(combined), axis=1, keepdims=True), 2.0**-100)
    e = jnp.floor(jnp.log2(largest) + 1e-4) - 14.0
    whole = jnp.round(combined * power(-e).astype(F32))
    out_ref[0, :tok, :] = whole.astype(jnp.int32).astype(jnp.int16)
    across = jnp.broadcast_to(e, (tok, tok)).T[:EXTRA]
    out_ref[0, tok:, :] = jnp.concatenate([across] * (combined.shape[1] // tok), axis=1).astype(jnp.int32).astype(jnp.int16)


def chunk_copy(coded_hbm, coded_ref, sems, i):
    many = coded_ref.shape[0] // sems.shape[0]
    part = pl.ds(i * many, many)
    return pltpu.make_async_copy(coded_hbm.at[part], coded_ref.at[part], sems.at[i])


def rows_and_scales(coded_ref, n, tok):
    coded = coded_ref[n].astype(jnp.int32).astype(F32)
    scale = power(coded[tok : tok + 1, :tok]).astype(F32)
    diagonal = jnp.where(iota((tok, tok), 0) == iota((tok, tok), 1), jnp.broadcast_to(scale, (tok, tok)), 0.0)
    return coded[:tok].astype(BF16), diagonal.astype(BF16)


def grad_kernel(coded_hbm, cot_ref, out_ref, total, coded_ref, sems):
    sources, chunks = coded_ref.shape[0], sems.shape[0]
    tok = cot_ref.shape[0] // sources
    many = sources // chunks
    for i in range(chunks):
        chunk_copy(coded_hbm, coded_ref, sems, i).start()
    total[...] = jnp.zeros_like(total)

    def step(i, carry):
        chunk_copy(coded_hbm, coded_ref, sems, i).wait()
        rows, cots = [], []
        for j in range(many):
            n = i * many + j
            coded, diagonal = rows_and_scales(coded_ref, n, tok)
            cot = cot_ref[pl.ds(pl.multiple_of(n * tok, tok), tok), :]
            rows.append(coded)
            cots.append(jnp.dot(diagonal, cot, preferred_element_type=F32).astype(BF16))
        total[...] += lax.dot_general(
            jnp.concatenate(cots), jnp.concatenate(rows), (((0,), (0,)), ((), ())), preferred_element_type=F32
        )
        return carry

    lax.fori_loop(0, chunks, step, 0)
    out_ref[...] = total[...].T.astype(BF16)


def mixed_kernel(coded_hbm, up_ref, out_ref, coded_ref, sems):
    sources, chunks = coded_ref.shape[0], sems.shape[0]
    tok = out_ref.shape[0] // sources
    many = sources // chunks
    for i in range(chunks):
        chunk_copy(coded_hbm, coded_ref, sems, i).start()
    ones = jnp.ones((tok, out_ref.shape[1]), BF16)

    def step(i, carry):
        chunk_copy(coded_hbm, coded_ref, sems, i).wait()
        for j in range(many):
            n = i * many + j
            coded, diagonal = rows_and_scales(coded_ref, n, tok)
            scale = jnp.dot(diagonal, ones, preferred_element_type=F32)
            mixed = jnp.dot(coded, up_ref[...], preferred_element_type=F32) * scale
            out_ref[pl.ds(pl.multiple_of(n * tok, tok), tok), :] = mixed.astype(BF16)
        return carry

    lax.fori_loop(0, chunks, step, 0)


def body(latent, up_proj, expert_in, expert_out, routes, gates, cotangent):
    n_expert = lax.axis_size("expert")
    n_dp = lax.axis_size("dp")
    tok, width = latent.shape
    cols = up_proj.shape[1]
    slots = n_expert * SLOTS
    sds = jax.ShapeDtypeStruct

    routes_t, gates_t = routes.T, gates.T
    outgoing = pl.pallas_call(
        dispatch_kernel, out_shape=sds((slots, width), BF16), in_specs=[VMEM] * 2, out_specs=VMEM, name="dispatch"
    )(routes_t, latent)
    weight = pl.pallas_call(
        weight_kernel, out_shape=sds((tok, slots), BF16), in_specs=[VMEM] * 2, out_specs=VMEM, name="weight"
    )(routes_t, gates_t)
    arrived = lax.all_to_all(
        outgoing.reshape(n_expert, SLOTS, width), "expert", split_axis=0, concat_axis=0, tiled=True
    ).reshape(slots, width)
    hidden = expert_out.shape[1]
    hbm = pl.BlockSpec(memory_space=pltpu.HBM)
    produced = pl.pallas_call(
        expert_kernel, out_shape=sds((slots, width), BF16), in_specs=[VMEM, hbm, hbm], out_specs=VMEM,
        scratch_shapes=[
            pltpu.VMEM((width, 2 * hidden), BF16),
            pltpu.VMEM((hidden, width), BF16),
            pltpu.SemaphoreType.DMA((4, 3)),
        ],
        compiler_params=LIMIT, name="expert",
    )(arrived, expert_in[0], expert_out[0])
    back = lax.all_to_all(
        produced.reshape(n_expert, SLOTS, width), "expert", split_axis=0, concat_axis=0, tiled=True
    ).reshape(slots, width)
    coded = pl.pallas_call(
        combine_kernel, out_shape=sds((1, tok + EXTRA, width), jnp.int16), in_specs=[VMEM] * 2, out_specs=VMEM,
        compiler_params=LIMIT, name="combine",
    )(weight, back)
    gathered = lax.all_gather(coded, "expert", axis=0, tiled=True)
    chunks = [pltpu.VMEM(gathered.shape, gathered.dtype), pltpu.SemaphoreType.DMA((n_expert // 4,))]
    grad = pl.pallas_call(
        grad_kernel, out_shape=sds((width, cols), BF16), in_specs=[hbm, VMEM], out_specs=VMEM,
        scratch_shapes=[pltpu.VMEM((cols, width), F32)] + chunks, compiler_params=LIMIT, name="grad",
    )(gathered, cotangent)
    mixed = pl.pallas_call(
        mixed_kernel, out_shape=sds(cotangent.shape, BF16), in_specs=[hbm, VMEM], out_specs=VMEM,
        scratch_shapes=chunks,
        compiler_params=LIMIT, name="mixed",
        cost_estimate=pl.CostEstimate(flops=2 * cotangent.shape[0] * width * cols, bytes_accessed=6 << 20, transcendentals=0),
    )(gathered, up_proj)

    parts = lax.all_to_all(grad.reshape(n_dp, width // n_dp, cols), "dp", split_axis=0, concat_axis=0, tiled=True)
    mine = jnp.sum(parts.astype(F32), axis=0)
    spread = jnp.broadcast_to(mine[None], (n_dp,) + mine.shape)
    grad_up = lax.all_to_all(spread, "dp", split_axis=0, concat_axis=0, tiled=True)
    return mixed, grad_up.reshape(width, cols)


def solution(mesh):
    in_specs = (
        P(("dp", "expert"), None),
        P(None, "expert"),
        P("expert", None, None),
        P("expert", None, None),
        P(("dp", "expert"), None),
        P(("dp", "expert"), None),
        P("dp", "expert"),
    )
    out_specs = (P("dp", "expert"), P(None, "expert"))
    return jax.shard_map(body, mesh=mesh, in_specs=in_specs, out_specs=out_specs, check_vma=False)
```

```python
import jax
import jax.numpy as jnp
from jax import lax
from jax.experimental import pallas as pl
from jax.experimental.pallas import tpu as pltpu
from jax.sharding import PartitionSpec as P

SLOTS = 14
LANES = 128
EXTRA = 8
BF16, F32 = jnp.bfloat16, jnp.float32
VMEM = pl.BlockSpec(memory_space=pltpu.VMEM)
HBM = pl.BlockSpec(memory_space=pltpu.HBM)


def vmem(mib):
    return pltpu.CompilerParams(vmem_limit_bytes=mib << 20)


def iota(shape, dim):
    return lax.broadcasted_iota(jnp.int32, shape, dim)


def slots_by_row(routes_t, n_expert):
    top, tok = routes_t.shape
    expert = iota((n_expert, tok), 0)
    member = jnp.zeros((n_expert, tok), F32)
    for k in range(top):
        member += jnp.where(routes_t[k : k + 1, :] == expert, 1.0, 0.0)
    earlier = jnp.where(iota((tok, tok), 0) < iota((tok, tok), 1), 1.0, 0.0).astype(BF16)
    slot = jnp.dot(member.astype(BF16), earlier, preferred_element_type=F32)
    slot = jnp.where(member > 0, slot, -1.0).astype(BF16)
    rows = n_expert * SLOTS
    spread = jnp.where(iota((rows, n_expert), 0) // SLOTS == iota((rows, n_expert), 1), 1.0, 0.0).astype(BF16)
    by_row = jnp.dot(spread, slot, preferred_element_type=F32)
    return by_row == (iota((rows, tok), 0) % SLOTS).astype(F32), spread


def pack(rows, wide_ref):
    n = rows.shape[1] // LANES
    for j in range(n):
        wide_ref[pl.ds(j, rows.shape[0], stride=n), :] = rows[:, j * LANES : (j + 1) * LANES]
    return wide_ref[...].astype(BF16)


def unpack(packed, wide_ref, n):
    wide_ref[...] = packed.astype(F32)
    rows = wide_ref.shape[0] // n
    return jnp.concatenate([wide_ref[pl.ds(j, rows, stride=n), :] for j in range(n)], axis=1).astype(BF16)


def dispatch_kernel(routes_ref, latent_ref, out_ref, wide_ref):
    n = latent_ref.shape[1] // LANES
    takes, _ = slots_by_row(routes_ref[...], out_ref.shape[0] // (SLOTS * n))
    rows = jnp.dot(jnp.where(takes, 1.0, 0.0).astype(BF16), latent_ref[...], preferred_element_type=F32)
    out_ref[...] = pack(rows, wide_ref)


def weight_kernel(routes_ref, gates_ref, out_ref):
    n_expert = out_ref.shape[1] // SLOTS
    routes_t, gates_t = routes_ref[...], gates_ref[...].astype(F32)
    takes, spread = slots_by_row(routes_t, n_expert)
    top, tok = routes_t.shape
    expert = iota((n_expert, tok), 0)
    gate = jnp.zeros((n_expert, tok), F32)
    for k in range(top):
        gate += jnp.where(routes_t[k : k + 1, :] == expert, gates_t[k : k + 1, :], 0.0)
    by_row = jnp.dot(spread, gate.astype(BF16), preferred_element_type=F32)
    out_ref[...] = jnp.where(takes, by_row, 0.0).T.astype(BF16)


def expert_kernel(x_ref, in_hbm, out_hbm, out_ref, in_ref, out_w_ref, wide_ref, sems):
    hidden, width = out_w_ref.shape
    step = hidden // sems.shape[0]
    copies = []
    for h in range(0, hidden, step):
        n = h // step
        gate, up = pl.ds(h, step), pl.ds(hidden + h, step)
        copies += [
            pltpu.make_async_copy(in_hbm.at[:, gate], in_ref.at[:, gate], sems.at[n, 0]),
            pltpu.make_async_copy(in_hbm.at[:, up], in_ref.at[:, up], sems.at[n, 1]),
            pltpu.make_async_copy(out_hbm.at[gate, :], out_w_ref.at[gate, :], sems.at[n, 2]),
        ]
    for copy in copies:
        copy.start()
    x = unpack(x_ref[...], wide_ref, width // LANES)
    total = jnp.zeros((x.shape[0], width), F32)
    for copy in copies[:2]:
        copy.wait()
    for h in range(0, hidden, step):
        g = jnp.dot(x, in_ref[:, h : h + step], preferred_element_type=F32)
        u = jnp.dot(x, in_ref[:, hidden + h : hidden + h + step], preferred_element_type=F32)
        if h == 0:
            for copy in copies[2:]:
                copy.wait()
        act = (g / (1.0 + jnp.exp(-g)) * u).astype(BF16)
        total += jnp.dot(act, out_w_ref[h : h + step, :], preferred_element_type=F32)
    out_ref[...] = pack(total, wide_ref)


def power(e):
    return jnp.exp2(e).astype(BF16)


def combine_kernel(w_ref, back_ref, out_ref, wide_ref):
    tok = w_ref.shape[0]
    back = unpack(back_ref[...], wide_ref, out_ref.shape[2] // LANES)
    combined = jnp.dot(w_ref[...], back, preferred_element_type=F32).astype(BF16).astype(F32)
    largest = jnp.maximum(jnp.max(jnp.abs(combined), axis=1, keepdims=True), 2.0**-100)
    e = jnp.floor(jnp.log2(largest) + 1e-4) - 14.0
    whole = jnp.round(combined * power(-e).astype(F32))
    across = jnp.broadcast_to(e, (tok, tok)).T[:EXTRA]
    across = jnp.concatenate([across] * (combined.shape[1] // tok), axis=1)
    out_ref[0] = jnp.concatenate([whole, across]).astype(jnp.int32).astype(jnp.int16)


def part_copy(hbm, ref, sems, i):
    many = ref.shape[0] // sems.shape[0]
    part = pl.ds(i * many, many)
    return pltpu.make_async_copy(hbm.at[part], ref.at[part], sems.at[i])


def rows_and_scales(coded_ref, n, tok):
    coded = coded_ref[n].astype(jnp.int32).astype(F32)
    scale = power(coded[tok : tok + 1, :tok]).astype(F32)
    diagonal = jnp.where(iota((tok, tok), 0) == iota((tok, tok), 1), jnp.broadcast_to(scale, (tok, tok)), 0.0)
    return coded[:tok].astype(BF16), diagonal.astype(BF16)


def grad_kernel(coded_hbm, cot_hbm, out_ref, coded_ref, cot_ref, coded_sems, cot_sems):
    sources, parts = coded_ref.shape[0], coded_sems.shape[0]
    tok = cot_ref.shape[0] // sources
    many = sources // parts
    for i in range(parts):
        part_copy(coded_hbm, coded_ref, coded_sems, i).start()
        part_copy(cot_hbm, cot_ref, cot_sems, i).start()
    total = None
    for i in range(parts):
        part_copy(coded_hbm, coded_ref, coded_sems, i).wait()
        part_copy(cot_hbm, cot_ref, cot_sems, i).wait()
        rows, cots = [], []
        for n in range(i * many, (i + 1) * many):
            coded, diagonal = rows_and_scales(coded_ref, n, tok)
            rows.append(coded)
            cots.append(jnp.dot(diagonal, cot_ref[n * tok : (n + 1) * tok, :], preferred_element_type=F32).astype(BF16))
        part = lax.dot_general(
            jnp.concatenate(cots), jnp.concatenate(rows), (((0,), (0,)), ((), ())), preferred_element_type=F32
        )
        total = part if total is None else total + part
    out_ref[...] = total.T.astype(BF16)


def mixed_kernel(coded_hbm, up_ref, out_hbm, coded_ref, out_ref, coded_sems, out_sems):
    sources, parts = coded_ref.shape[0], coded_sems.shape[0]
    tok = out_ref.shape[0] // sources
    many = sources // parts
    ones = jnp.ones((tok, out_ref.shape[1]), BF16)
    for i in range(parts):
        part_copy(coded_hbm, coded_ref, coded_sems, i).start()
    for i in range(parts):
        part_copy(coded_hbm, coded_ref, coded_sems, i).wait()
        for n in range(i * many, (i + 1) * many):
            coded, diagonal = rows_and_scales(coded_ref, n, tok)
            scale = jnp.dot(diagonal, ones, preferred_element_type=F32)
            mixed = jnp.dot(coded, up_ref[...], preferred_element_type=F32) * scale
            out_ref[n * tok : (n + 1) * tok, :] = mixed.astype(BF16)
        part_copy(out_ref, out_hbm, out_sems, i).start()
    for i in range(parts):
        part_copy(out_ref, out_hbm, out_sems, i).wait()


def body(latent, up_proj, expert_in, expert_out, routes, gates, cotangent):
    n_expert = lax.axis_size("expert")
    n_dp = lax.axis_size("dp")
    tok, width = latent.shape
    cols = up_proj.shape[1]
    slots = n_expert * SLOTS
    sds = jax.ShapeDtypeStruct

    routes_t, gates_t = routes.T, gates.T
    hidden = expert_out.shape[1]
    packed = sds((slots * width // LANES, LANES), BF16)
    wide = pltpu.VMEM(packed.shape, F32)
    per_expert = (n_expert, packed.shape[0] // n_expert, LANES)
    outgoing = pl.pallas_call(
        dispatch_kernel, out_shape=packed, in_specs=[VMEM] * 2, out_specs=VMEM, scratch_shapes=[wide],
        compiler_params=vmem(60), name="dispatch",
    )(routes_t, latent)
    weight = pl.pallas_call(
        weight_kernel, out_shape=sds((tok, slots), BF16), in_specs=[VMEM] * 2, out_specs=VMEM,
        compiler_params=vmem(8), name="weight",
    )(routes_t, gates_t)
    arrived = lax.all_to_all(
        outgoing.reshape(per_expert), "expert", split_axis=0, concat_axis=0, tiled=True
    ).reshape(packed.shape)
    produced = pl.pallas_call(
        expert_kernel, out_shape=packed, in_specs=[VMEM, HBM, HBM], out_specs=VMEM,
        scratch_shapes=[
            pltpu.VMEM((width, 2 * hidden), BF16),
            pltpu.VMEM((hidden, width), BF16),
            wide,
            pltpu.SemaphoreType.DMA((2, 3)),
        ],
        compiler_params=vmem(60), name="expert",
    )(arrived, expert_in[0], expert_out[0])
    back = lax.all_to_all(
        produced.reshape(per_expert), "expert", split_axis=0, concat_axis=0, tiled=True
    ).reshape(packed.shape)
    coded = pl.pallas_call(
        combine_kernel, out_shape=sds((1, tok + EXTRA, width), jnp.int16), in_specs=[VMEM] * 2, out_specs=VMEM,
        scratch_shapes=[wide], compiler_params=vmem(8), name="combine",
    )(weight, back)
    gathered = lax.all_gather(coded, "expert", axis=0, tiled=True)
    parts = n_expert // 8
    coded_parts = [pltpu.VMEM(gathered.shape, gathered.dtype)]
    sems = [pltpu.SemaphoreType.DMA((parts,))] * 2
    whole = [pltpu.VMEM(cotangent.shape, BF16)]
    grad = pl.pallas_call(
        grad_kernel, out_shape=sds((width, cols), BF16), in_specs=[HBM, HBM], out_specs=VMEM,
        scratch_shapes=coded_parts + whole + sems, compiler_params=vmem(60), name="grad",
    )(gathered, cotangent)
    mixed = pl.pallas_call(
        mixed_kernel, out_shape=sds(cotangent.shape, BF16), in_specs=[HBM, VMEM], out_specs=HBM,
        scratch_shapes=coded_parts + whole + sems, compiler_params=vmem(60), name="mixed",
        cost_estimate=pl.CostEstimate(flops=2 * cotangent.shape[0] * width * cols, bytes_accessed=6 << 20, transcendentals=0),
    )(gathered, up_proj)

    parts = lax.all_to_all(grad.reshape(n_dp, width // n_dp, cols), "dp", split_axis=0, concat_axis=0, tiled=True)
    parts, mixed = lax.optimization_barrier((parts, mixed))
    mine = jnp.sum(parts.astype(F32), axis=0).astype(BF16)
    spread = jnp.broadcast_to(mine[None], (n_dp,) + mine.shape)
    grad_up = lax.all_to_all(spread, "dp", split_axis=0, concat_axis=0, tiled=True).astype(F32)
    return mixed, grad_up.reshape(width, cols)


def solution(mesh):
    in_specs = (
        P(("dp", "expert"), None),
        P(None, "expert"),
        P("expert", None, None),
        P("expert", None, None),
        P(("dp", "expert"), None),
        P(("dp", "expert"), None),
        P("dp", "expert"),
    )
    out_specs = (P("dp", "expert"), P(None, "expert"))
    return jax.shard_map(body, mesh=mesh, in_specs=in_specs, out_specs=out_specs, check_vma=False)
```

```python
import jax
import jax.numpy as jnp
from jax import lax
from jax.experimental import pallas as pl
from jax.experimental.pallas import tpu as pltpu
from jax.sharding import PartitionSpec as P

SLOTS = 13
LANES = 128
EXTRA = 8
BF16, F32 = jnp.bfloat16, jnp.float32
VMEM = pl.BlockSpec(memory_space=pltpu.VMEM)
HBM = pl.BlockSpec(memory_space=pltpu.HBM)


def vmem(mib):
    return pltpu.CompilerParams(vmem_limit_bytes=mib << 20)


def iota(shape, dim):
    return lax.broadcasted_iota(jnp.int32, shape, dim)


def slots_by_row(routes_t, n_expert):
    top, tok = routes_t.shape
    expert = iota((n_expert, tok), 0)
    member = jnp.zeros((n_expert, tok), F32)
    for k in range(top):
        member += jnp.where(routes_t[k : k + 1, :] == expert, 1.0, 0.0)
    earlier = jnp.where(iota((tok, tok), 0) < iota((tok, tok), 1), 1.0, 0.0).astype(BF16)
    slot = jnp.dot(member.astype(BF16), earlier, preferred_element_type=F32)
    slot = jnp.where(member > 0, slot, -1.0).astype(BF16)
    rows = n_expert * SLOTS
    spread = jnp.where(iota((rows, n_expert), 0) // SLOTS == iota((rows, n_expert), 1), 1.0, 0.0).astype(BF16)
    by_row = jnp.dot(spread, slot, preferred_element_type=F32)
    return by_row == (iota((rows, tok), 0) % SLOTS).astype(F32), spread


def pack(rows, wide_ref):
    n = rows.shape[1] // LANES
    for j in range(n):
        wide_ref[pl.ds(j, rows.shape[0], stride=n), :] = rows[:, j * LANES : (j + 1) * LANES]
    return wide_ref[...].astype(BF16)


def unpack(packed, wide_ref, n):
    wide_ref[...] = packed.astype(F32)
    rows = wide_ref.shape[0] // n
    return jnp.concatenate([wide_ref[pl.ds(j, rows, stride=n), :] for j in range(n)], axis=1).astype(BF16)


def dispatch_kernel(routes_ref, latent_ref, out_ref, wide_ref):
    n = latent_ref.shape[1] // LANES
    takes, _ = slots_by_row(routes_ref[...], out_ref.shape[0] // (SLOTS * n))
    rows = jnp.dot(jnp.where(takes, 1.0, 0.0).astype(BF16), latent_ref[...], preferred_element_type=F32)
    out_ref[...] = pack(rows, wide_ref)


def weight_kernel(routes_ref, gates_ref, out_ref):
    n_expert = out_ref.shape[1] // SLOTS
    routes_t, gates_t = routes_ref[...], gates_ref[...].astype(F32)
    takes, spread = slots_by_row(routes_t, n_expert)
    top, tok = routes_t.shape
    expert = iota((n_expert, tok), 0)
    gate = jnp.zeros((n_expert, tok), F32)
    for k in range(top):
        gate += jnp.where(routes_t[k : k + 1, :] == expert, gates_t[k : k + 1, :], 0.0)
    by_row = jnp.dot(spread, gate.astype(BF16), preferred_element_type=F32)
    out_ref[...] = jnp.where(takes, by_row, 0.0).T.astype(BF16)


def expert_kernel(x_ref, in_ref, out_w_ref, out_ref, wide_ref):
    hidden, width = out_w_ref.shape
    step = 512
    x = unpack(x_ref[...], wide_ref, width // LANES)
    total = jnp.zeros((x.shape[0], width), F32)
    for h in range(0, hidden, step):
        g = jnp.dot(x, in_ref[:, h : h + step], preferred_element_type=F32)
        u = jnp.dot(x, in_ref[:, hidden + h : hidden + h + step], preferred_element_type=F32)
        act = (g / (1.0 + jnp.exp(-g)) * u).astype(BF16)
        total += jnp.dot(act, out_w_ref[h : h + step, :], preferred_element_type=F32)
    out_ref[...] = pack(total, wide_ref)


def power(e):
    return jnp.exp2(e).astype(BF16)


def combine_kernel(w_ref, back_ref, out_ref, wide_ref):
    tok = w_ref.shape[0]
    back = unpack(back_ref[...], wide_ref, out_ref.shape[2] // LANES)
    combined = jnp.dot(w_ref[...], back, preferred_element_type=F32).astype(BF16).astype(F32)
    largest = jnp.maximum(jnp.max(jnp.abs(combined), axis=1, keepdims=True), 2.0**-100)
    e = jnp.floor(jnp.log2(largest) + 1e-4) - 14.0
    whole = jnp.round(combined * power(-e).astype(F32))
    across = jnp.broadcast_to(e, (tok, tok)).T[:EXTRA]
    across = jnp.concatenate([across] * (combined.shape[1] // tok), axis=1)
    out_ref[0] = jnp.concatenate([whole, across]).astype(jnp.int32).astype(jnp.int16)


def part_copy(hbm, ref, sems, i):
    many = ref.shape[0] // sems.shape[0]
    part = pl.ds(i * many, many)
    return pltpu.make_async_copy(hbm.at[part], ref.at[part], sems.at[i])


def rows_and_scales(coded_ref, n, tok):
    coded = coded_ref[n].astype(jnp.int32).astype(F32)
    scale = power(coded[tok : tok + 1, :tok]).astype(F32)
    diagonal = jnp.where(iota((tok, tok), 0) == iota((tok, tok), 1), jnp.broadcast_to(scale, (tok, tok)), 0.0)
    return coded[:tok].astype(BF16), diagonal.astype(BF16)


def grad_kernel(coded_hbm, cot_hbm, out_ref, coded_ref, cot_ref, coded_sems, cot_sems):
    sources, parts = coded_ref.shape[0], coded_sems.shape[0]
    tok = cot_ref.shape[0] // sources
    many = sources // parts
    for i in range(parts):
        part_copy(coded_hbm, coded_ref, coded_sems, i).start()
        part_copy(cot_hbm, cot_ref, cot_sems, i).start()
    total = None
    for i in range(parts):
        part_copy(coded_hbm, coded_ref, coded_sems, i).wait()
        part_copy(cot_hbm, cot_ref, cot_sems, i).wait()
        rows, cots = [], []
        for n in range(i * many, (i + 1) * many):
            coded, diagonal = rows_and_scales(coded_ref, n, tok)
            rows.append(coded)
            cots.append(jnp.dot(diagonal, cot_ref[n * tok : (n + 1) * tok, :], preferred_element_type=F32).astype(BF16))
        part = lax.dot_general(
            jnp.concatenate(cots), jnp.concatenate(rows), (((0,), (0,)), ((), ())), preferred_element_type=F32
        )
        total = part if total is None else total + part
    out_ref[...] = total.T.astype(BF16)


def mixed_kernel(coded_hbm, up_ref, out_hbm, coded_ref, out_ref, coded_sems, out_sems):
    sources, parts = coded_ref.shape[0], coded_sems.shape[0]
    tok = out_ref.shape[0] // sources
    many = sources // parts
    ones = jnp.ones((tok, out_ref.shape[1]), BF16)
    for i in range(parts):
        part_copy(coded_hbm, coded_ref, coded_sems, i).start()
    for i in range(parts):
        part_copy(coded_hbm, coded_ref, coded_sems, i).wait()
        for n in range(i * many, (i + 1) * many):
            coded, diagonal = rows_and_scales(coded_ref, n, tok)
            scale = jnp.dot(diagonal, ones, preferred_element_type=F32)
            mixed = jnp.dot(coded, up_ref[...], preferred_element_type=F32) * scale
            out_ref[n * tok : (n + 1) * tok, :] = mixed.astype(BF16)
        part_copy(out_ref, out_hbm, out_sems, i).start()
    for i in range(parts):
        part_copy(out_ref, out_hbm, out_sems, i).wait()


def body(latent, up_proj, expert_in, expert_out, routes, gates, cotangent):
    n_expert = lax.axis_size("expert")
    n_dp = lax.axis_size("dp")
    tok, width = latent.shape
    cols = up_proj.shape[1]
    slots = n_expert * SLOTS
    sds = jax.ShapeDtypeStruct

    routes_t, gates_t = routes.T, gates.T
    hidden = expert_out.shape[1]
    packed = sds((slots * width // LANES, LANES), BF16)
    wide = pltpu.VMEM(packed.shape, F32)
    per_expert = (n_expert, SLOTS, width // LANES, LANES)
    outgoing = pl.pallas_call(
        dispatch_kernel, out_shape=packed, in_specs=[VMEM] * 2, out_specs=VMEM, scratch_shapes=[wide],
        compiler_params=vmem(8), name="dispatch",
        cost_estimate=pl.CostEstimate(flops=6000000000, bytes_accessed=10000000, transcendentals=0),
    )(routes_t, latent)
    weight = pl.pallas_call(
        weight_kernel, out_shape=sds((tok, slots), BF16), in_specs=[VMEM] * 2, out_specs=VMEM,
        compiler_params=vmem(8), name="weight",
    )(routes_t, gates_t)
    arrived = lax.all_to_all(
        outgoing.reshape(per_expert), "expert", split_axis=0, concat_axis=0, tiled=True
    ).reshape(packed.shape)
    produced = pl.pallas_call(
        expert_kernel, out_shape=packed, in_specs=[VMEM] * 3, out_specs=VMEM, scratch_shapes=[wide],
        compiler_params=vmem(20), name="expert",
    )(arrived, expert_in[0], expert_out[0])
    back = lax.all_to_all(
        produced.reshape(per_expert), "expert", split_axis=0, concat_axis=0, tiled=True
    ).reshape(packed.shape)
    coded = pl.pallas_call(
        combine_kernel, out_shape=sds((1, tok + EXTRA, width), jnp.int16), in_specs=[VMEM] * 2, out_specs=VMEM,
        scratch_shapes=[wide], compiler_params=vmem(8), name="combine",
    )(weight, back)
    gathered = lax.all_gather(coded, "expert", axis=0, tiled=True)
    parts = n_expert // 8
    coded_parts = [pltpu.VMEM(gathered.shape, gathered.dtype)]
    sems = [pltpu.SemaphoreType.DMA((parts,))] * 2
    whole = [pltpu.VMEM(cotangent.shape, BF16)]
    grad = pl.pallas_call(
        grad_kernel, out_shape=sds((width, cols), BF16), in_specs=[HBM, HBM], out_specs=VMEM,
        scratch_shapes=coded_parts + whole + sems, compiler_params=vmem(60), name="grad",
    )(gathered, cotangent)
    mixed = pl.pallas_call(
        mixed_kernel, out_shape=sds(cotangent.shape, BF16), in_specs=[HBM, VMEM], out_specs=HBM,
        scratch_shapes=coded_parts + whole + sems, compiler_params=vmem(60), name="mixed",
        cost_estimate=pl.CostEstimate(flops=2 * cotangent.shape[0] * width * cols, bytes_accessed=6 << 20, transcendentals=0),
    )(gathered, up_proj)

    parts = lax.all_to_all(grad.reshape(n_dp, width // n_dp, cols), "dp", split_axis=0, concat_axis=0, tiled=True)
    parts, mixed = lax.optimization_barrier((parts, mixed))
    mine = jnp.sum(parts.astype(F32), axis=0).astype(BF16)
    spread = jnp.broadcast_to(mine[None], (n_dp,) + mine.shape)
    grad_up = lax.all_to_all(spread, "dp", split_axis=0, concat_axis=0, tiled=True).astype(F32)
    return mixed, grad_up.reshape(width, cols)


def solution(mesh):
    in_specs = (
        P(("dp", "expert"), None),
        P(None, "expert"),
        P("expert", None, None),
        P("expert", None, None),
        P(("dp", "expert"), None),
        P(("dp", "expert"), None),
        P("dp", "expert"),
    )
    out_specs = (P("dp", "expert"), P(None, "expert"))
    return jax.shard_map(body, mesh=mesh, in_specs=in_specs, out_specs=out_specs, check_vma=False)
```

```python
import jax
import jax.numpy as jnp
from jax import lax
from jax.experimental import pallas as pl
from jax.experimental.pallas import tpu as pltpu
from jax.sharding import PartitionSpec as P

SLOTS = 13
LANES = 128
EXTRA = 8
BF16, F32 = jnp.bfloat16, jnp.float32
VMEM = pl.BlockSpec(memory_space=pltpu.VMEM)
HBM = pl.BlockSpec(memory_space=pltpu.HBM)


def vmem(mib):
    return pltpu.CompilerParams(vmem_limit_bytes=mib << 20)


def iota(shape, dim):
    return lax.broadcasted_iota(jnp.int32, shape, dim)


def slots_by_row(routes_t, n_expert):
    top, tok = routes_t.shape
    expert = iota((n_expert, tok), 0)
    member = jnp.zeros((n_expert, tok), F32)
    for k in range(top):
        member += jnp.where(routes_t[k : k + 1, :] == expert, 1.0, 0.0)
    earlier = jnp.where(iota((tok, tok), 0) < iota((tok, tok), 1), 1.0, 0.0).astype(BF16)
    slot = jnp.dot(member.astype(BF16), earlier, preferred_element_type=F32)
    slot = jnp.where(member > 0, slot, -1.0).astype(BF16)
    rows = n_expert * SLOTS
    spread = jnp.where(iota((rows, n_expert), 0) // SLOTS == iota((rows, n_expert), 1), 1.0, 0.0).astype(BF16)
    by_row = jnp.dot(spread, slot, preferred_element_type=F32)
    return by_row == (iota((rows, tok), 0) % SLOTS).astype(F32), spread


def pack(rows, wide_ref):
    n = rows.shape[1] // LANES
    for j in range(n):
        wide_ref[pl.ds(j, rows.shape[0], stride=n), :] = rows[:, j * LANES : (j + 1) * LANES]
    return wide_ref[...].astype(BF16)


def unpack(packed, wide_ref, n):
    wide_ref[...] = packed.astype(F32)
    rows = wide_ref.shape[0] // n
    return jnp.concatenate([wide_ref[pl.ds(j, rows, stride=n), :] for j in range(n)], axis=1).astype(BF16)


def dispatch_kernel(routes_ref, latent_ref, out_ref, wide_ref):
    n = latent_ref.shape[1] // LANES
    takes, _ = slots_by_row(routes_ref[...], out_ref.shape[0] // (SLOTS * n))
    rows = jnp.dot(jnp.where(takes, 1.0, 0.0).astype(BF16), latent_ref[...], preferred_element_type=F32)
    out_ref[...] = pack(rows, wide_ref)


def weight_kernel(routes_ref, gates_ref, out_ref):
    n_expert = out_ref.shape[1] // SLOTS
    routes_t, gates_t = routes_ref[...], gates_ref[...].astype(F32)
    takes, spread = slots_by_row(routes_t, n_expert)
    top, tok = routes_t.shape
    expert = iota((n_expert, tok), 0)
    gate = jnp.zeros((n_expert, tok), F32)
    for k in range(top):
        gate += jnp.where(routes_t[k : k + 1, :] == expert, gates_t[k : k + 1, :], 0.0)
    by_row = jnp.dot(spread, gate.astype(BF16), preferred_element_type=F32)
    out_ref[...] = jnp.where(takes, by_row, 0.0).T.astype(BF16)


def expert_kernel(x_ref, in_ref, out_w_ref, out_ref, wide_ref):
    hidden, width = out_w_ref.shape
    step = 512
    x = unpack(x_ref[...], wide_ref, width // LANES)
    total = jnp.zeros((x.shape[0], width), F32)
    for h in range(0, hidden, step):
        g = jnp.dot(x, in_ref[:, h : h + step], preferred_element_type=F32)
        u = jnp.dot(x, in_ref[:, hidden + h : hidden + h + step], preferred_element_type=F32)
        act = (g / (1.0 + jnp.exp(-g)) * u).astype(BF16)
        total += jnp.dot(act, out_w_ref[h : h + step, :], preferred_element_type=F32)
    out_ref[...] = pack(total, wide_ref)


def power(e):
    return jnp.exp2(e).astype(BF16)


def combine_kernel(w_ref, back_ref, out_ref, wide_ref):
    tok = w_ref.shape[0]
    back = unpack(back_ref[...], wide_ref, out_ref.shape[2] // LANES)
    combined = jnp.dot(w_ref[...], back, preferred_element_type=F32).astype(BF16).astype(F32)
    largest = jnp.maximum(jnp.max(jnp.abs(combined), axis=1, keepdims=True), 2.0**-100)
    e = jnp.floor(jnp.log2(largest) + 1e-4) - 14.0
    whole = jnp.round(combined * power(-e).astype(F32))
    across = jnp.broadcast_to(e, (tok, tok)).T[:EXTRA]
    across = jnp.concatenate([across] * (combined.shape[1] // tok), axis=1)
    out_ref[0] = jnp.concatenate([whole, across]).astype(jnp.int32).astype(jnp.int16)


def part_copy(hbm, ref, sems, i):
    many = ref.shape[0] // sems.shape[0]
    part = pl.ds(i * many, many)
    return pltpu.make_async_copy(hbm.at[part], ref.at[part], sems.at[i])


def rows_and_scales(coded_ref, n, tok):
    coded = coded_ref[n].astype(jnp.int32).astype(F32)
    scale = power(coded[tok : tok + 1, :tok]).astype(F32)
    diagonal = jnp.where(iota((tok, tok), 0) == iota((tok, tok), 1), jnp.broadcast_to(scale, (tok, tok)), 0.0)
    return coded[:tok].astype(BF16), diagonal.astype(BF16)


def grad_kernel(coded_ref, cot_hbm, out_ref, coded_hbm, cot_ref, coded_sem, cot_sems):
    sources, parts = coded_ref.shape[0], cot_sems.shape[0]
    tok = cot_ref.shape[0] // sources
    many = sources // parts
    for i in range(parts):
        part_copy(cot_hbm, cot_ref, cot_sems, i).start()
    keep = pltpu.make_async_copy(coded_ref, coded_hbm.at[pl.ds(0, sources)], coded_sem)
    keep.start()
    total = None
    for i in range(parts):
        part_copy(cot_hbm, cot_ref, cot_sems, i).wait()
        rows, cots = [], []
        for n in range(i * many, (i + 1) * many):
            coded, diagonal = rows_and_scales(coded_ref, n, tok)
            rows.append(coded)
            cots.append(jnp.dot(diagonal, cot_ref[n * tok : (n + 1) * tok, :], preferred_element_type=F32).astype(BF16))
        part = lax.dot_general(
            jnp.concatenate(cots), jnp.concatenate(rows), (((0,), (0,)), ((), ())), preferred_element_type=F32
        )
        total = part if total is None else total + part
    out_ref[...] = total.T.astype(BF16)
    keep.wait()


def mixed_kernel(coded_hbm, up_ref, out_hbm, coded_ref, out_ref, coded_sems, out_sems):
    sources, parts = coded_ref.shape[0], coded_sems.shape[0]
    tok = out_ref.shape[0] // sources
    many = sources // parts
    ones = jnp.ones((tok, out_ref.shape[1]), BF16)
    for i in range(parts):
        part_copy(coded_hbm, coded_ref, coded_sems, i).start()
    for i in range(parts):
        part_copy(coded_hbm, coded_ref, coded_sems, i).wait()
        for n in range(i * many, (i + 1) * many):
            coded, diagonal = rows_and_scales(coded_ref, n, tok)
            scale = jnp.dot(diagonal, ones, preferred_element_type=F32)
            mixed = jnp.dot(coded, up_ref[...], preferred_element_type=F32) * scale
            out_ref[n * tok : (n + 1) * tok, :] = mixed.astype(BF16)
        part_copy(out_ref, out_hbm, out_sems, i).start()
    for i in range(parts):
        part_copy(out_ref, out_hbm, out_sems, i).wait()


def body(latent, up_proj, expert_in, expert_out, routes, gates, cotangent):
    n_expert = lax.axis_size("expert")
    n_dp = lax.axis_size("dp")
    tok, width = latent.shape
    cols = up_proj.shape[1]
    slots = n_expert * SLOTS
    sds = jax.ShapeDtypeStruct

    routes_t, gates_t = routes.T, gates.T
    hidden = expert_out.shape[1]
    packed = sds((slots * width // LANES, LANES), BF16)
    wide = pltpu.VMEM(packed.shape, F32)
    per_expert = (n_expert, SLOTS, width // LANES, LANES)
    outgoing = pl.pallas_call(
        dispatch_kernel, out_shape=packed, in_specs=[VMEM] * 2, out_specs=VMEM, scratch_shapes=[wide],
        compiler_params=vmem(8), name="dispatch",
        cost_estimate=pl.CostEstimate(flops=6000000000, bytes_accessed=10000000, transcendentals=0),
    )(routes_t, latent)
    weight = pl.pallas_call(
        weight_kernel, out_shape=sds((tok, slots), BF16), in_specs=[VMEM] * 2, out_specs=VMEM,
        compiler_params=vmem(8), name="weight",
    )(routes_t, gates_t)
    arrived = lax.all_to_all(
        outgoing.reshape(per_expert), "expert", split_axis=0, concat_axis=0, tiled=True
    ).reshape(packed.shape)
    produced = pl.pallas_call(
        expert_kernel, out_shape=packed, in_specs=[VMEM] * 3, out_specs=VMEM, scratch_shapes=[wide],
        compiler_params=vmem(20), name="expert",
    )(arrived, expert_in[0], expert_out[0])
    back = lax.all_to_all(
        produced.reshape(per_expert), "expert", split_axis=0, concat_axis=0, tiled=True
    ).reshape(packed.shape)
    coded = pl.pallas_call(
        combine_kernel, out_shape=sds((1, tok + EXTRA, width), jnp.int16), in_specs=[VMEM] * 2, out_specs=VMEM,
        scratch_shapes=[wide], compiler_params=vmem(8), name="combine",
    )(weight, back)
    gathered = lax.all_gather(coded, "expert", axis=0, tiled=True)
    parts = n_expert // 8
    coded_parts = [pltpu.VMEM(gathered.shape, gathered.dtype)]
    sems = [pltpu.SemaphoreType.DMA((parts,))] * 2
    whole = [pltpu.VMEM(cotangent.shape, BF16)]
    room = sds((2 * n_expert,) + gathered.shape[1:], gathered.dtype)
    grad, kept = pl.pallas_call(
        grad_kernel, out_shape=[sds((width, cols), BF16), room],
        in_specs=[VMEM, HBM], out_specs=[VMEM, HBM],
        scratch_shapes=whole + [pltpu.SemaphoreType.DMA, sems[0]], compiler_params=vmem(47), name="grad",
    )(gathered, cotangent)
    mixed = pl.pallas_call(
        mixed_kernel, out_shape=sds(cotangent.shape, BF16), in_specs=[HBM, VMEM], out_specs=HBM,
        scratch_shapes=coded_parts + whole + sems, compiler_params=vmem(60), name="mixed",
        cost_estimate=pl.CostEstimate(flops=2 * cotangent.shape[0] * width * cols, bytes_accessed=6 << 20, transcendentals=0),
    )(kept, up_proj)

    parts = lax.all_to_all(grad.reshape(n_dp, width // n_dp, cols), "dp", split_axis=0, concat_axis=0, tiled=True)
    parts, mixed = lax.optimization_barrier((parts, mixed))
    mine = jnp.sum(parts.astype(F32), axis=0).astype(BF16)
    spread = jnp.broadcast_to(mine[None], (n_dp,) + mine.shape)
    grad_up = lax.all_to_all(spread, "dp", split_axis=0, concat_axis=0, tiled=True).astype(F32)
    return mixed, grad_up.reshape(width, cols)


def solution(mesh):
    in_specs = (
        P(("dp", "expert"), None),
        P(None, "expert"),
        P("expert", None, None),
        P("expert", None, None),
        P(("dp", "expert"), None),
        P(("dp", "expert"), None),
        P("dp", "expert"),
    )
    out_specs = (P("dp", "expert"), P(None, "expert"))
    return jax.shard_map(body, mesh=mesh, in_specs=in_specs, out_specs=out_specs, check_vma=False)
```

```python
import jax
import jax.numpy as jnp
from jax import lax
from jax.experimental import pallas as pl
from jax.experimental.pallas import tpu as pltpu
from jax.sharding import PartitionSpec as P

SLOTS = 13
LANES = 128
EXTRA = 8
BF16, F32 = jnp.bfloat16, jnp.float32
VMEM = pl.BlockSpec(memory_space=pltpu.VMEM)
HBM = pl.BlockSpec(memory_space=pltpu.HBM)


def vmem(mib):
    return pltpu.CompilerParams(vmem_limit_bytes=mib << 20)


def iota(shape, dim):
    return lax.broadcasted_iota(jnp.int32, shape, dim)


def slots_by_row(routes_t, n_expert):
    top, tok = routes_t.shape
    expert = iota((n_expert, tok), 0)
    member = jnp.zeros((n_expert, tok), F32)
    for k in range(top):
        member += jnp.where(routes_t[k : k + 1, :] == expert, 1.0, 0.0)
    earlier = jnp.where(iota((tok, tok), 0) < iota((tok, tok), 1), 1.0, 0.0).astype(BF16)
    slot = jnp.dot(member.astype(BF16), earlier, preferred_element_type=F32)
    slot = jnp.where(member > 0, slot, -1.0).astype(BF16)
    rows = n_expert * SLOTS
    spread = jnp.where(iota((rows, n_expert), 0) // SLOTS == iota((rows, n_expert), 1), 1.0, 0.0).astype(BF16)
    by_row = jnp.dot(spread, slot, preferred_element_type=F32)
    return by_row == (iota((rows, tok), 0) % SLOTS).astype(F32), spread


def pack(rows, wide_ref):
    n = rows.shape[1] // LANES
    for j in range(n):
        wide_ref[pl.ds(j, rows.shape[0], stride=n), :] = rows[:, j * LANES : (j + 1) * LANES]
    return wide_ref[...].astype(BF16)


def unpack(packed, wide_ref, n):
    wide_ref[...] = packed.astype(F32)
    rows = wide_ref.shape[0] // n
    return jnp.concatenate([wide_ref[pl.ds(j, rows, stride=n), :] for j in range(n)], axis=1).astype(BF16)


def dispatch_kernel(routes_ref, latent_ref, out_ref, wide_ref):
    n = latent_ref.shape[1] // LANES
    takes, _ = slots_by_row(routes_ref[...], out_ref.shape[0] // (SLOTS * n))
    rows = jnp.dot(jnp.where(takes, 1.0, 0.0).astype(BF16), latent_ref[...], preferred_element_type=F32)
    out_ref[...] = pack(rows, wide_ref)


def weight_kernel(routes_ref, gates_ref, out_ref):
    n_expert = out_ref.shape[1] // SLOTS
    routes_t, gates_t = routes_ref[...], gates_ref[...].astype(F32)
    takes, spread = slots_by_row(routes_t, n_expert)
    top, tok = routes_t.shape
    expert = iota((n_expert, tok), 0)
    gate = jnp.zeros((n_expert, tok), F32)
    for k in range(top):
        gate += jnp.where(routes_t[k : k + 1, :] == expert, gates_t[k : k + 1, :], 0.0)
    by_row = jnp.dot(spread, gate.astype(BF16), preferred_element_type=F32)
    out_ref[...] = jnp.where(takes, by_row, 0.0).T.astype(BF16)


def expert_kernel(x_ref, in_ref, out_w_ref, out_ref, wide_ref):
    hidden, width = out_w_ref.shape
    step = 512
    x = unpack(x_ref[...], wide_ref, width // LANES)
    total = jnp.zeros((x.shape[0], width), F32)
    for h in range(0, hidden, step):
        g = jnp.dot(x, in_ref[:, h : h + step], preferred_element_type=F32)
        u = jnp.dot(x, in_ref[:, hidden + h : hidden + h + step], preferred_element_type=F32)
        act = (g / (1.0 + jnp.exp(-g)) * u).astype(BF16)
        total += jnp.dot(act, out_w_ref[h : h + step, :], preferred_element_type=F32)
    out_ref[...] = pack(total, wide_ref)


def power(e):
    return jnp.exp2(e).astype(BF16)


def combine_kernel(w_ref, back_ref, out_ref, wide_ref):
    tok = w_ref.shape[0]
    back = unpack(back_ref[...], wide_ref, wide_ref.shape[0] // w_ref.shape[1])
    combined = jnp.dot(w_ref[...], back, preferred_element_type=F32).astype(BF16).astype(F32)
    largest = jnp.maximum(jnp.max(jnp.abs(combined), axis=1, keepdims=True), 2.0**-100)
    e = jnp.floor(jnp.log2(largest) + 1e-4) - 14.0
    whole = jnp.round(combined * power(-e).astype(F32))
    across = jnp.broadcast_to(e, (tok, tok)).T[:EXTRA]
    slabs = [whole[:, j : j + LANES] for j in range(0, whole.shape[1], LANES)]
    out_ref[0] = jnp.concatenate(slabs + [across]).astype(jnp.int32).astype(jnp.int16)


def part_copy(hbm, ref, sems, i):
    many = ref.shape[0] // sems.shape[0]
    part = pl.ds(i * many, many)
    return pltpu.make_async_copy(hbm.at[part], ref.at[part], sems.at[i])


def rows_and_scales(coded_ref, n, tok):
    coded = coded_ref[n].astype(jnp.int32).astype(F32)
    end = coded.shape[0] - EXTRA
    scale = power(coded[end : end + 1]).astype(F32)
    diagonal = jnp.where(iota((tok, tok), 0) == iota((tok, tok), 1), jnp.broadcast_to(scale, (tok, tok)), 0.0)
    rows = jnp.concatenate([coded[j : j + tok] for j in range(0, end, tok)], axis=1)
    return rows.astype(BF16), diagonal.astype(BF16)


def grad_kernel(coded_ref, cot_hbm, out_ref, coded_hbm, cot_ref, coded_sem, cot_sems):
    sources, parts = coded_ref.shape[0], cot_sems.shape[0]
    tok = cot_ref.shape[0] // sources
    many = sources // parts
    for i in range(parts):
        part_copy(cot_hbm, cot_ref, cot_sems, i).start()
    keep = pltpu.make_async_copy(coded_ref, coded_hbm.at[pl.ds(0, sources)], coded_sem)
    keep.start()
    total = None
    for i in range(parts):
        part_copy(cot_hbm, cot_ref, cot_sems, i).wait()
        rows, cots = [], []
        for n in range(i * many, (i + 1) * many):
            coded, diagonal = rows_and_scales(coded_ref, n, tok)
            rows.append(coded)
            cots.append(jnp.dot(diagonal, cot_ref[n * tok : (n + 1) * tok, :], preferred_element_type=F32).astype(BF16))
        part = lax.dot_general(
            jnp.concatenate(cots), jnp.concatenate(rows), (((0,), (0,)), ((), ())), preferred_element_type=F32
        )
        total = part if total is None else total + part
    out_ref[...] = total.T.astype(BF16)
    keep.wait()


def mixed_kernel(coded_hbm, up_ref, out_hbm, coded_ref, out_ref, coded_sems, out_sems):
    sources, parts = coded_ref.shape[0], coded_sems.shape[0]
    tok = out_ref.shape[0] // sources
    many = sources // parts
    ones = jnp.ones((tok, out_ref.shape[1]), BF16)
    for i in range(parts):
        part_copy(coded_hbm, coded_ref, coded_sems, i).start()
    for i in range(parts):
        part_copy(coded_hbm, coded_ref, coded_sems, i).wait()
        for n in range(i * many, (i + 1) * many):
            coded, diagonal = rows_and_scales(coded_ref, n, tok)
            scale = jnp.dot(diagonal, ones, preferred_element_type=F32)
            mixed = jnp.dot(coded, up_ref[...], preferred_element_type=F32) * scale
            out_ref[n * tok : (n + 1) * tok, :] = mixed.astype(BF16)
        part_copy(out_ref, out_hbm, out_sems, i).start()
    for i in range(parts):
        part_copy(out_ref, out_hbm, out_sems, i).wait()


def body(latent, up_proj, expert_in, expert_out, routes, gates, cotangent):
    n_expert = lax.axis_size("expert")
    n_dp = lax.axis_size("dp")
    tok, width = latent.shape
    cols = up_proj.shape[1]
    slots = n_expert * SLOTS
    sds = jax.ShapeDtypeStruct

    routes_t, gates_t = routes.T, gates.T
    hidden = expert_out.shape[1]
    packed = sds((slots * width // LANES, LANES), BF16)
    wide = pltpu.VMEM(packed.shape, F32)
    per_expert = (n_expert, SLOTS, width // LANES, LANES)
    outgoing = pl.pallas_call(
        dispatch_kernel, out_shape=packed, in_specs=[VMEM] * 2, out_specs=VMEM, scratch_shapes=[wide],
        compiler_params=vmem(8), name="dispatch",
        cost_estimate=pl.CostEstimate(flops=6000000000, bytes_accessed=10000000, transcendentals=0),
    )(routes_t, latent)
    weight = pl.pallas_call(
        weight_kernel, out_shape=sds((tok, slots), BF16), in_specs=[VMEM] * 2, out_specs=VMEM,
        compiler_params=vmem(8), name="weight",
    )(routes_t, gates_t)
    arrived = lax.all_to_all(
        outgoing.reshape(per_expert), "expert", split_axis=0, concat_axis=0, tiled=True
    ).reshape(packed.shape)
    produced = pl.pallas_call(
        expert_kernel, out_shape=packed, in_specs=[VMEM] * 3, out_specs=VMEM, scratch_shapes=[wide],
        compiler_params=vmem(20), name="expert",
    )(arrived, expert_in[0], expert_out[0])
    back = lax.all_to_all(
        produced.reshape(per_expert), "expert", split_axis=0, concat_axis=0, tiled=True
    ).reshape(packed.shape)
    coded = pl.pallas_call(
        combine_kernel, out_shape=sds((1, tok * width // LANES + EXTRA, LANES), jnp.int16), in_specs=[VMEM] * 2, out_specs=VMEM,
        scratch_shapes=[wide], compiler_params=vmem(8), name="combine",
    )(weight, back)
    gathered = lax.all_gather(coded, "expert", axis=0, tiled=True)
    parts = n_expert // 8
    coded_parts = [pltpu.VMEM(gathered.shape, gathered.dtype)]
    sems = [pltpu.SemaphoreType.DMA((parts,))] * 2
    whole = [pltpu.VMEM(cotangent.shape, BF16)]
    room = sds((2 * n_expert,) + gathered.shape[1:], gathered.dtype)
    grad, kept = pl.pallas_call(
        grad_kernel, out_shape=[sds((width, cols), BF16), room],
        in_specs=[VMEM, HBM], out_specs=[VMEM, HBM],
        scratch_shapes=whole + [pltpu.SemaphoreType.DMA, sems[0]], compiler_params=vmem(47), name="grad",
    )(gathered, cotangent)
    mixed = pl.pallas_call(
        mixed_kernel, out_shape=sds(cotangent.shape, BF16), in_specs=[HBM, VMEM], out_specs=HBM,
        scratch_shapes=coded_parts + whole + sems, compiler_params=vmem(60), name="mixed",
        cost_estimate=pl.CostEstimate(flops=2 * cotangent.shape[0] * width * cols, bytes_accessed=6 << 20, transcendentals=0),
    )(kept, up_proj)

    parts = lax.all_to_all(grad.reshape(n_dp, width // n_dp, cols), "dp", split_axis=0, concat_axis=0, tiled=True)
    parts, mixed = lax.optimization_barrier((parts, mixed))
    mine = jnp.sum(parts.astype(F32), axis=0).astype(BF16)
    spread = jnp.broadcast_to(mine[None], (n_dp,) + mine.shape)
    grad_up = lax.all_to_all(spread, "dp", split_axis=0, concat_axis=0, tiled=True).astype(F32)
    return mixed, grad_up.reshape(width, cols)


def solution(mesh):
    in_specs = (
        P(("dp", "expert"), None),
        P(None, "expert"),
        P("expert", None, None),
        P("expert", None, None),
        P(("dp", "expert"), None),
        P(("dp", "expert"), None),
        P("dp", "expert"),
    )
    out_specs = (P("dp", "expert"), P(None, "expert"))
    return jax.shard_map(body, mesh=mesh, in_specs=in_specs, out_specs=out_specs, check_vma=False)
```

```python
import jax
import jax.numpy as jnp
from jax import lax
from jax.experimental import pallas as pl
from jax.experimental.pallas import tpu as pltpu
from jax.sharding import PartitionSpec as P

SLOTS = 13
LANES = 128
EXTRA = 8
BF16, F32 = jnp.bfloat16, jnp.float32
VMEM = pl.BlockSpec(memory_space=pltpu.VMEM)
HBM = pl.BlockSpec(memory_space=pltpu.HBM)


def vmem(mib):
    return pltpu.CompilerParams(vmem_limit_bytes=mib << 20)


def iota(shape, dim):
    return lax.broadcasted_iota(jnp.int32, shape, dim)


def slots_by_row(routes_t, n_expert):
    top, tok = routes_t.shape
    expert = iota((n_expert, tok), 0)
    member = jnp.zeros((n_expert, tok), F32)
    for k in range(top):
        member += jnp.where(routes_t[k : k + 1, :] == expert, 1.0, 0.0)
    earlier = jnp.where(iota((tok, tok), 0) < iota((tok, tok), 1), 1.0, 0.0).astype(BF16)
    slot = jnp.dot(member.astype(BF16), earlier, preferred_element_type=F32)
    slot = jnp.where(member > 0, slot, -1.0).astype(BF16)
    rows = n_expert * SLOTS
    spread = jnp.where(iota((rows, n_expert), 0) // SLOTS == iota((rows, n_expert), 1), 1.0, 0.0).astype(BF16)
    by_row = jnp.dot(spread, slot, preferred_element_type=F32)
    return by_row == (iota((rows, tok), 0) % SLOTS).astype(F32), spread


def pack(rows, wide_ref):
    n = rows.shape[1] // LANES
    for j in range(n):
        wide_ref[pl.ds(j, rows.shape[0], stride=n), :] = rows[:, j * LANES : (j + 1) * LANES]
    return wide_ref[...].astype(BF16)


def unpack(packed, wide_ref, n):
    wide_ref[...] = packed.astype(F32)
    rows = wide_ref.shape[0] // n
    return jnp.concatenate([wide_ref[pl.ds(j, rows, stride=n), :] for j in range(n)], axis=1).astype(BF16)


def dispatch_kernel(routes_ref, latent_ref, out_ref, wide_ref):
    n = latent_ref.shape[1] // LANES
    takes, _ = slots_by_row(routes_ref[...], out_ref.shape[0] // (SLOTS * n))
    rows = jnp.dot(jnp.where(takes, 1.0, 0.0).astype(BF16), latent_ref[...], preferred_element_type=F32)
    out_ref[...] = pack(rows, wide_ref)


def weight_kernel(routes_ref, gates_ref, out_ref):
    n_expert = out_ref.shape[1] // SLOTS
    routes_t, gates_t = routes_ref[...], gates_ref[...].astype(F32)
    takes, spread = slots_by_row(routes_t, n_expert)
    top, tok = routes_t.shape
    expert = iota((n_expert, tok), 0)
    gate = jnp.zeros((n_expert, tok), F32)
    for k in range(top):
        gate += jnp.where(routes_t[k : k + 1, :] == expert, gates_t[k : k + 1, :], 0.0)
    by_row = jnp.dot(spread, gate.astype(BF16), preferred_element_type=F32)
    out_ref[...] = jnp.where(takes, by_row, 0.0).T.astype(BF16)


def expert_kernel(x_ref, in_ref, out_w_ref, out_ref, wide_ref):
    hidden, width = out_w_ref.shape
    step = 512
    x = unpack(x_ref[...], wide_ref, width // LANES)
    total = jnp.zeros((x.shape[0], width), F32)
    for h in range(0, hidden, step):
        g = jnp.dot(x, in_ref[:, h : h + step], preferred_element_type=F32)
        u = jnp.dot(x, in_ref[:, hidden + h : hidden + h + step], preferred_element_type=F32)
        act = (g / (1.0 + jnp.exp(-g)) * u).astype(BF16)
        total += jnp.dot(act, out_w_ref[h : h + step, :], preferred_element_type=F32)
    out_ref[...] = pack(total, wide_ref)


def power(e):
    return jnp.exp2(e).astype(BF16)


def combine_kernel(w_ref, back_ref, out_ref, wide_ref):
    tok = w_ref.shape[0]
    back = unpack(back_ref[...], wide_ref, wide_ref.shape[0] // w_ref.shape[1])
    combined = jnp.dot(w_ref[...], back, preferred_element_type=F32).astype(BF16).astype(F32)
    largest = jnp.maximum(jnp.max(jnp.abs(combined), axis=1, keepdims=True), 2.0**-100)
    e = jnp.floor(jnp.log2(largest) + 1e-4) - 14.0
    whole = jnp.round(combined * power(-e).astype(F32))
    across = jnp.broadcast_to(e, (tok, tok)).T[:EXTRA]
    slabs = [whole[:, j : j + LANES] for j in range(0, whole.shape[1], LANES)]
    out_ref[0] = jnp.concatenate(slabs + [across]).astype(jnp.int32).astype(jnp.int16)


def part_copy(hbm, ref, sems, i):
    many = ref.shape[0] // sems.shape[0]
    part = pl.ds(i * many, many)
    return pltpu.make_async_copy(hbm.at[part], ref.at[part], sems.at[i])


def rows_and_scales(coded_ref, n, tok):
    coded = coded_ref[n].astype(jnp.int32).astype(F32)
    end = coded.shape[0] - EXTRA
    scale = power(coded[end : end + 1]).astype(F32)
    diagonal = jnp.where(iota((tok, tok), 0) == iota((tok, tok), 1), jnp.broadcast_to(scale, (tok, tok)), 0.0)
    rows = jnp.concatenate([coded[j : j + tok] for j in range(0, end, tok)], axis=1)
    return rows.astype(BF16), diagonal.astype(BF16)


def grad_kernel(coded_ref, cot_ref, out_ref, coded_hbm, coded_sem):
    sources = coded_ref.shape[0]
    tok = cot_ref.shape[0] // sources
    many = 8
    keep = pltpu.make_async_copy(coded_ref, coded_hbm.at[pl.ds(0, sources)], coded_sem)
    keep.start()
    total = None
    for i in range(sources // many):
        rows, cots = [], []
        for n in range(i * many, (i + 1) * many):
            coded, diagonal = rows_and_scales(coded_ref, n, tok)
            rows.append(coded)
            cots.append(jnp.dot(diagonal, cot_ref[n * tok : (n + 1) * tok, :], preferred_element_type=F32).astype(BF16))
        part = lax.dot_general(
            jnp.concatenate(cots), jnp.concatenate(rows), (((0,), (0,)), ((), ())), preferred_element_type=F32
        )
        total = part if total is None else total + part
    out_ref[...] = total.T.astype(BF16)
    keep.wait()


def mixed_kernel(coded_hbm, up_ref, out_hbm, coded_ref, out_ref, coded_sems, out_sems):
    sources, parts = coded_ref.shape[0], coded_sems.shape[0]
    tok = out_ref.shape[0] // sources
    many = sources // parts
    ones = jnp.ones((tok, out_ref.shape[1]), BF16)
    for i in range(parts):
        part_copy(coded_hbm, coded_ref, coded_sems, i).start()
    for i in range(parts):
        part_copy(coded_hbm, coded_ref, coded_sems, i).wait()
        for n in range(i * many, (i + 1) * many):
            coded, diagonal = rows_and_scales(coded_ref, n, tok)
            scale = jnp.dot(diagonal, ones, preferred_element_type=F32)
            mixed = jnp.dot(coded, up_ref[...], preferred_element_type=F32) * scale
            out_ref[n * tok : (n + 1) * tok, :] = mixed.astype(BF16)
        part_copy(out_ref, out_hbm, out_sems, i).start()
    for i in range(parts):
        part_copy(out_ref, out_hbm, out_sems, i).wait()


def sum_kernel(parts_ref, out_ref):
    total = jnp.sum(parts_ref[...].astype(F32), axis=0).astype(BF16)
    out_ref[...] = jnp.broadcast_to(total[None], out_ref.shape)


def body(latent, up_proj, expert_in, expert_out, routes, gates, cotangent):
    n_expert = lax.axis_size("expert")
    n_dp = lax.axis_size("dp")
    tok, width = latent.shape
    cols = up_proj.shape[1]
    slots = n_expert * SLOTS
    sds = jax.ShapeDtypeStruct

    routes_t, gates_t = routes.T, gates.T
    hidden = expert_out.shape[1]
    packed = sds((slots * width // LANES, LANES), BF16)
    wide = pltpu.VMEM(packed.shape, F32)
    per_expert = (n_expert, SLOTS, width // LANES, LANES)
    outgoing = pl.pallas_call(
        dispatch_kernel, out_shape=packed, in_specs=[VMEM] * 2, out_specs=VMEM, scratch_shapes=[wide],
        compiler_params=vmem(8), name="dispatch",
        cost_estimate=pl.CostEstimate(flops=6000000000, bytes_accessed=10000000, transcendentals=0),
    )(routes_t, latent)
    weight = pl.pallas_call(
        weight_kernel, out_shape=sds((tok, slots), BF16), in_specs=[VMEM] * 2, out_specs=VMEM,
        compiler_params=vmem(8), name="weight",
    )(routes_t, gates_t)
    arrived = lax.all_to_all(
        outgoing.reshape(per_expert), "expert", split_axis=0, concat_axis=0, tiled=True
    ).reshape(packed.shape)
    produced = pl.pallas_call(
        expert_kernel, out_shape=packed, in_specs=[VMEM] * 3, out_specs=VMEM, scratch_shapes=[wide],
        compiler_params=vmem(20), name="expert",
    )(arrived, expert_in[0], expert_out[0])
    back = lax.all_to_all(
        produced.reshape(per_expert), "expert", split_axis=0, concat_axis=0, tiled=True
    ).reshape(packed.shape)
    coded = pl.pallas_call(
        combine_kernel, out_shape=sds((1, tok * width // LANES + EXTRA, LANES), jnp.int16), in_specs=[VMEM] * 2, out_specs=VMEM,
        scratch_shapes=[wide], compiler_params=vmem(8), name="combine",
    )(weight, back)
    gathered = lax.all_gather(coded, "expert", axis=0, tiled=True)
    parts = n_expert // 8
    coded_parts = [pltpu.VMEM(gathered.shape, gathered.dtype)]
    sems = [pltpu.SemaphoreType.DMA((parts,))] * 2
    whole = [pltpu.VMEM(cotangent.shape, BF16)]
    room = sds((2 * n_expert,) + gathered.shape[1:], gathered.dtype)
    grad, kept = pl.pallas_call(
        grad_kernel, out_shape=[sds((width, cols), BF16), room],
        in_specs=[VMEM] * 2, out_specs=[VMEM, HBM],
        scratch_shapes=[pltpu.SemaphoreType.DMA], compiler_params=vmem(47), name="grad",
    )(gathered, cotangent)
    mixed = pl.pallas_call(
        mixed_kernel, out_shape=sds(cotangent.shape, BF16), in_specs=[HBM, VMEM], out_specs=HBM,
        scratch_shapes=coded_parts + whole + sems, compiler_params=vmem(60), name="mixed",
        cost_estimate=pl.CostEstimate(flops=2 * cotangent.shape[0] * width * cols, bytes_accessed=6 << 20, transcendentals=0),
    )(kept, up_proj)

    parts = lax.all_to_all(grad.reshape(n_dp, width // n_dp, cols), "dp", split_axis=0, concat_axis=0, tiled=True)
    parts, mixed = lax.optimization_barrier((parts, mixed))
    spread = pl.pallas_call(
        sum_kernel, out_shape=sds(parts.shape, BF16), in_specs=[VMEM], out_specs=VMEM,
        compiler_params=vmem(8), name="sum",
    )(parts)
    grad_up = lax.all_to_all(spread, "dp", split_axis=0, concat_axis=0, tiled=True).astype(F32)
    return mixed, grad_up.reshape(width, cols)


def solution(mesh):
    in_specs = (
        P(("dp", "expert"), None),
        P(None, "expert"),
        P("expert", None, None),
        P("expert", None, None),
        P(("dp", "expert"), None),
        P(("dp", "expert"), None),
        P("dp", "expert"),
    )
    out_specs = (P("dp", "expert"), P(None, "expert"))
    return jax.shard_map(body, mesh=mesh, in_specs=in_specs, out_specs=out_specs, check_vma=False)
```

```python
import functools

import jax
import jax.numpy as jnp
from jax import lax
from jax.experimental import pallas as pl
from jax.experimental.pallas import tpu as pltpu
from jax.sharding import PartitionSpec as P

SLOTS = 13
LANES = 128
EXTRA = 8
BF16, F32 = jnp.bfloat16, jnp.float32
VMEM = pl.BlockSpec(memory_space=pltpu.VMEM)
HBM = pl.BlockSpec(memory_space=pltpu.HBM)


def vmem(mib):
    return pltpu.CompilerParams(vmem_limit_bytes=mib << 20)


def iota(shape, dim):
    return lax.broadcasted_iota(jnp.int32, shape, dim)


def slots_by_row(routes_t, n_expert):
    top, tok = routes_t.shape
    expert = iota((n_expert, tok), 0)
    member = jnp.zeros((n_expert, tok), F32)
    for k in range(top):
        member += jnp.where(routes_t[k : k + 1, :] == expert, 1.0, 0.0)
    earlier = jnp.where(iota((tok, tok), 0) < iota((tok, tok), 1), 1.0, 0.0).astype(BF16)
    slot = jnp.dot(member.astype(BF16), earlier, preferred_element_type=F32)
    slot = jnp.where(member > 0, slot, -1.0).astype(BF16)
    rows = n_expert * SLOTS
    spread = jnp.where(iota((rows, n_expert), 0) // SLOTS == iota((rows, n_expert), 1), 1.0, 0.0).astype(BF16)
    by_row = jnp.dot(spread, slot, preferred_element_type=F32)
    return by_row == (iota((rows, tok), 0) % SLOTS).astype(F32), spread


def pack(rows, wide_ref):
    n = rows.shape[1] // LANES
    for j in range(n):
        wide_ref[pl.ds(j, rows.shape[0], stride=n), :] = rows[:, j * LANES : (j + 1) * LANES]
    return wide_ref[...].astype(BF16)


def unpack(packed, wide_ref, n):
    wide_ref[...] = packed.astype(F32)
    rows = wide_ref.shape[0] // n
    return jnp.concatenate([wide_ref[pl.ds(j, rows, stride=n), :] for j in range(n)], axis=1).astype(BF16)


def dispatch_kernel(routes_ref, latent_ref, out_ref, wide_ref):
    n = latent_ref.shape[1] // LANES
    takes, _ = slots_by_row(routes_ref[...], out_ref.shape[0] // (SLOTS * n))
    rows = jnp.dot(jnp.where(takes, 1.0, 0.0).astype(BF16), latent_ref[...], preferred_element_type=F32)
    out_ref[...] = pack(rows, wide_ref)


def weight_kernel(routes_ref, gates_ref, out_ref):
    n_expert = out_ref.shape[1] // SLOTS
    routes_t, gates_t = routes_ref[...], gates_ref[...].astype(F32)
    takes, spread = slots_by_row(routes_t, n_expert)
    top, tok = routes_t.shape
    expert = iota((n_expert, tok), 0)
    gate = jnp.zeros((n_expert, tok), F32)
    for k in range(top):
        gate += jnp.where(routes_t[k : k + 1, :] == expert, gates_t[k : k + 1, :], 0.0)
    by_row = jnp.dot(spread, gate.astype(BF16), preferred_element_type=F32)
    out_ref[...] = jnp.where(takes, by_row, 0.0).T.astype(BF16)


def expert_kernel(x_ref, in_ref, out_w_ref, out_ref, wide_ref):
    hidden, width = out_w_ref.shape
    step = 512
    x = unpack(x_ref[...], wide_ref, width // LANES)
    total = jnp.zeros((x.shape[0], width), F32)
    for h in range(0, hidden, step):
        g = jnp.dot(x, in_ref[:, h : h + step], preferred_element_type=F32)
        u = jnp.dot(x, in_ref[:, hidden + h : hidden + h + step], preferred_element_type=F32)
        act = (g / (1.0 + jnp.exp(-g)) * u).astype(BF16)
        total += jnp.dot(act, out_w_ref[h : h + step, :], preferred_element_type=F32)
    out_ref[...] = pack(total, wide_ref)


def power(e):
    return jnp.exp2(e).astype(BF16)


def combine_kernel(w_ref, back_ref, out_ref, wide_ref):
    tok = w_ref.shape[0]
    back = unpack(back_ref[...], wide_ref, wide_ref.shape[0] // w_ref.shape[1])
    combined = jnp.dot(w_ref[...], back, preferred_element_type=F32).astype(BF16).astype(F32)
    largest = jnp.maximum(jnp.max(jnp.abs(combined), axis=1, keepdims=True), 2.0**-100)
    e = jnp.floor(jnp.log2(largest) + 1e-4) - 14.0
    whole = jnp.round(combined * power(-e).astype(F32))
    across = jnp.broadcast_to(e, (tok, tok)).T[:EXTRA]
    slabs = [whole[:, j : j + LANES] for j in range(0, whole.shape[1], LANES)]
    out_ref[0] = jnp.concatenate(slabs + [across]).astype(jnp.int32).astype(jnp.int16)


def part_copy(hbm, ref, sems, i):
    many = ref.shape[0] // sems.shape[0]
    part = pl.ds(i * many, many)
    return pltpu.make_async_copy(hbm.at[part], ref.at[part], sems.at[i])


def rows_and_scales(coded_ref, n, tok):
    coded = coded_ref[n].astype(jnp.int32).astype(F32)
    end = coded.shape[0] - EXTRA
    scale = power(coded[end : end + 1]).astype(F32)
    diagonal = jnp.where(iota((tok, tok), 0) == iota((tok, tok), 1), jnp.broadcast_to(scale, (tok, tok)), 0.0)
    rows = jnp.concatenate([coded[j : j + tok] for j in range(0, end, tok)], axis=1)
    return rows.astype(BF16), diagonal.astype(BF16)


def grad_kernel(coded_ref, cot_ref, out_ref, coded_hbm, coded_sem):
    sources = coded_ref.shape[0]
    tok = cot_ref.shape[0] // sources
    many = 8
    keep = pltpu.make_async_copy(coded_ref, coded_hbm.at[pl.ds(0, sources)], coded_sem)
    keep.start()
    total = None
    for i in range(sources // many):
        rows, cots = [], []
        for n in range(i * many, (i + 1) * many):
            coded, diagonal = rows_and_scales(coded_ref, n, tok)
            rows.append(coded)
            cots.append(jnp.dot(diagonal, cot_ref[n * tok : (n + 1) * tok, :], preferred_element_type=F32).astype(BF16))
        part = lax.dot_general(
            jnp.concatenate(cots), jnp.concatenate(rows), (((0,), (0,)), ((), ())), preferred_element_type=F32
        )
        total = part if total is None else total + part
    out_ref[...] = total.T.astype(BF16)
    keep.wait()


def mixed_kernel(mine, coded_hbm, up_ref, *rest):
    out_hbm, coded_ref, out_ref, coded_sems, out_sems = rest[-5:]
    sources, parts = coded_ref.shape[0], coded_sems.shape[0]
    tok = out_ref.shape[0] // sources
    many = sources // parts
    ones = jnp.ones((tok, out_ref.shape[1]), BF16)
    for i in mine:
        part_copy(coded_hbm, coded_ref, coded_sems, i).start()
    for i in mine:
        part_copy(coded_hbm, coded_ref, coded_sems, i).wait()
        for n in range(i * many, (i + 1) * many):
            coded, diagonal = rows_and_scales(coded_ref, n, tok)
            scale = jnp.dot(diagonal, ones, preferred_element_type=F32)
            mixed = jnp.dot(coded, up_ref[...], preferred_element_type=F32) * scale
            out_ref[n * tok : (n + 1) * tok, :] = mixed.astype(BF16)
        part_copy(out_ref, out_hbm, out_sems, i).start()
    for i in mine:
        part_copy(out_ref, out_hbm, out_sems, i).wait()


def sum_kernel(parts_ref, out_ref):
    total = jnp.sum(parts_ref[...].astype(F32), axis=0).astype(BF16)
    out_ref[...] = jnp.broadcast_to(total[None], out_ref.shape)


def body(latent, up_proj, expert_in, expert_out, routes, gates, cotangent):
    n_expert = lax.axis_size("expert")
    n_dp = lax.axis_size("dp")
    tok, width = latent.shape
    cols = up_proj.shape[1]
    slots = n_expert * SLOTS
    sds = jax.ShapeDtypeStruct

    routes_t, gates_t = routes.T, gates.T
    hidden = expert_out.shape[1]
    packed = sds((slots * width // LANES, LANES), BF16)
    wide = pltpu.VMEM(packed.shape, F32)
    per_expert = (n_expert, SLOTS, width // LANES, LANES)
    outgoing = pl.pallas_call(
        dispatch_kernel, out_shape=packed, in_specs=[VMEM] * 2, out_specs=VMEM, scratch_shapes=[wide],
        compiler_params=vmem(8), name="dispatch",
        cost_estimate=pl.CostEstimate(flops=6000000000, bytes_accessed=10000000, transcendentals=0),
    )(routes_t, latent)
    weight = pl.pallas_call(
        weight_kernel, out_shape=sds((tok, slots), BF16), in_specs=[VMEM] * 2, out_specs=VMEM,
        compiler_params=vmem(8), name="weight",
    )(routes_t, gates_t)
    arrived = lax.all_to_all(
        outgoing.reshape(per_expert), "expert", split_axis=0, concat_axis=0, tiled=True
    ).reshape(packed.shape)
    produced = pl.pallas_call(
        expert_kernel, out_shape=packed, in_specs=[VMEM] * 3, out_specs=VMEM, scratch_shapes=[wide],
        compiler_params=vmem(20), name="expert",
    )(arrived, expert_in[0], expert_out[0])
    back = lax.all_to_all(
        produced.reshape(per_expert), "expert", split_axis=0, concat_axis=0, tiled=True
    ).reshape(packed.shape)
    coded = pl.pallas_call(
        combine_kernel, out_shape=sds((1, tok * width // LANES + EXTRA, LANES), jnp.int16), in_specs=[VMEM] * 2, out_specs=VMEM,
        scratch_shapes=[wide], compiler_params=vmem(8), name="combine",
    )(weight, back)
    gathered = lax.all_gather(coded, "expert", axis=0, tiled=True)
    parts = n_expert // 8
    coded_parts = [pltpu.VMEM(gathered.shape, gathered.dtype)]
    sems = [pltpu.SemaphoreType.DMA((parts,))] * 2
    whole = [pltpu.VMEM(cotangent.shape, BF16)]
    room = sds((2 * n_expert,) + gathered.shape[1:], gathered.dtype)
    grad, kept = pl.pallas_call(
        grad_kernel, out_shape=[sds((width, cols), BF16), room],
        in_specs=[VMEM] * 2, out_specs=[VMEM, HBM],
        scratch_shapes=[pltpu.SemaphoreType.DMA], compiler_params=vmem(47), name="grad",
    )(gathered, cotangent)
    def project(mine, kept, *before):
        return pl.pallas_call(
            functools.partial(mixed_kernel, mine), out_shape=sds(cotangent.shape, BF16),
            in_specs=[HBM, VMEM] + [HBM] * len(before), out_specs=HBM,
            scratch_shapes=coded_parts + whole + sems, compiler_params=vmem(60), name=f"mixed{mine[0]}",
            input_output_aliases={2: 0} if before else {},
            cost_estimate=pl.CostEstimate(
                flops=cotangent.shape[0] * width * cols, bytes_accessed=3 << 20, transcendentals=0
            ),
        )(kept, up_proj, *before)

    mixed = project(range(parts // 2), kept)

    summands = lax.all_to_all(grad.reshape(n_dp, width // n_dp, cols), "dp", split_axis=0, concat_axis=0, tiled=True)
    summands, mixed = lax.optimization_barrier((summands, mixed))
    spread = pl.pallas_call(
        sum_kernel, out_shape=sds(summands.shape, BF16), in_specs=[VMEM], out_specs=VMEM,
        compiler_params=vmem(8), name="sum",
    )(summands)
    spread, kept = lax.optimization_barrier((spread, kept))
    mixed = project(range(parts // 2, parts), kept, mixed)
    grad_up = lax.all_to_all(spread, "dp", split_axis=0, concat_axis=0, tiled=True).astype(F32)
    return mixed, grad_up.reshape(width, cols)


def solution(mesh):
    in_specs = (
        P(("dp", "expert"), None),
        P(None, "expert"),
        P("expert", None, None),
        P("expert", None, None),
        P(("dp", "expert"), None),
        P(("dp", "expert"), None),
        P("dp", "expert"),
    )
    out_specs = (P("dp", "expert"), P(None, "expert"))
    return jax.shard_map(body, mesh=mesh, in_specs=in_specs, out_specs=out_specs, check_vma=False)
```
